512 devices in a mesh: section: 64 (over y, z), rep: 8 (over x, core).
Axes of the slice: x: 4, y: 8, z: 8, core: 2. Of those that a mesh axis runs over, the one named last changes fastest.
Arguments:
- node_features: bfloat16 [65536, 256], P(('section', 'rep')), may hold values from -6 to 6
- tile_values: bfloat16 [8192, 128, 128], P(('section', 'rep')), may hold values from -0.5 to 0.5
- tile_rows: int32 [8192], P(('section', 'rep')), may hold values from 0 to 7
- tile_cols: int32 [8192], P(('section', 'rep')), may hold values from 0 to 63
- tile_counts: int32 [512], P(('section', 'rep')), may hold values from 1 to 16, as said below
- cheb_weights: bfloat16 [768, 256], replicated, may hold values from -0.21875 to 0.21875
- bias: float32 [256], replicated, may hold values from -3 to 3
- out_cotangent: bfloat16 [65536, 256], P(('section', 'rep')), may hold values from -0.0625 to 0.0625
Outputs:
- layer_out: bfloat16 [65536, 256], P(('section', 'rep'))
- weight_grads: float32 [768, 256], replicated
The draws below stay inside these ranges and needn't reach their ends.
Inputs may be any that keep to these rules, and one draw needn't show every extreme that they name: `tile_counts`: some device holds exactly 16 live tiles; the busiest devices hold about twice the mean.
All inputs are finite; a program needn't handle non-finite values.
Results may differ from the reference program's by a relative error of at most 0.0067.
Values may be sent and summed in bfloat16 or wider, within the bound.
A program may use at most 64 MiB of HBM per device.

```python
import jax
import jax.numpy as jnp
from jax import lax

BLOCK = 128
F = 256
BLOCKS_DEV = 1
TCAP = 16
GROUPS = 512
SLOTS = 8192
SECTION_BLOCKS = 8
SOURCE_BLOCKS = 64
NODES = 65536
CHEB_IN = 768
N_REP = 8


def draw_tile_counts(key, part):
    base_key, order_key = jax.random.split(jax.random.fold_in(key, 17))
    lowest = max(1, TCAP // 8)
    base = jax.random.randint(base_key, (GROUPS,), lowest, TCAP * 5 // 8 + 1)
    order = jax.random.permutation(order_key, GROUPS)
    heavy = order < max(1, GROUPS // 8)
    return jnp.where(heavy, TCAP, base).astype(jnp.int32)


def with_ends(values, key, smallest, largest):
    longest = values.shape.index(max(values.shape))
    spots = []
    for shift in (0, 1):
        where = [jax.random.randint(jax.random.fold_in(key, axis), (), 0, length) for axis, length in enumerate(values.shape)]
        where[longest] = (where[longest] + shift) % values.shape[longest]
        spots.append(tuple(where))
    return values.at[spots[0]].set(smallest).at[spots[1]].set(largest)


def block_scale(own_key, extent, pieces, low, top_value):
    level = 1.0
    for dim, blocks in pieces:
        steps = jax.random.uniform(jax.random.fold_in(jax.random.fold_in(own_key, 6), dim), (blocks,), jnp.float32, low / len(pieces), top_value / len(pieces))
        level = level * jnp.repeat(jnp.exp(steps), extent[dim] // blocks).reshape((-1,) + (1,) * (len(extent) - 1 - dim))
    return level


def gaussian(stream_key, dims, deviation, most, shards=(), held_as=jnp.bfloat16):
    gain = block_scale(stream_key, dims, shards, -0.22, 0.18) if shards else 1.0
    values = jax.random.normal(stream_key, dims, jnp.float32) * deviation * gain
    return jnp.minimum(jnp.maximum(values, -most), most).astype(held_as)


def setup_inputs(seed: int = 0) -> dict:
    arg_keys = jax.random.split(jax.random.key(seed), 9)
    return {
        "node_features": gaussian(arg_keys[0], (NODES, F), 1.0, 6.0, ((0, 512),)),
        "tile_values": gaussian(arg_keys[1], (SLOTS, BLOCK, BLOCK), (1.0 / (8 * BLOCK) ** 0.5), 0.5, ((0, 512),)),
        "tile_rows": with_ends(jax.random.randint(arg_keys[2], (SLOTS,), 0, SECTION_BLOCKS), jax.random.fold_in(arg_keys[2], 1), 0, SECTION_BLOCKS - 1).astype(jnp.int32),
        "tile_cols": with_ends(jax.random.randint(arg_keys[3], (SLOTS,), 0, SOURCE_BLOCKS), jax.random.fold_in(arg_keys[3], 1), 0, SOURCE_BLOCKS - 1).astype(jnp.int32),
        "tile_counts": draw_tile_counts(jax.random.fold_in(arg_keys[8], 71), 0),
        "cheb_weights": gaussian(arg_keys[5], (CHEB_IN, F), CHEB_IN ** -0.5, 0.21875),
        "bias": gaussian(arg_keys[6], (F,), 0.5, 3.0, (), jnp.float32),
        "out_cotangent": gaussian(arg_keys[7], (NODES, F), (1.0 / NODES ** 0.5), 0.0625, ((0, 512),)),
    }


def smooth_gate(values):
    return jax.nn.gelu(values, approximate=True)

def apply_operator(features, tile_values, tile_rows, tile_cols, tile_counts):
    node_blocks = features.reshape(-1, BLOCK, F)
    tiles = tile_values.reshape(GROUPS, TCAP, BLOCK, BLOCK)
    rows_all = tile_rows.reshape(GROUPS, TCAP).astype(jnp.int32)
    cols_all = tile_cols.reshape(GROUPS, TCAP).astype(jnp.int32)
    slot_ids = jnp.arange(TCAP, dtype=jnp.int32)

    def visit(total, group):
        section_id = (group // N_REP).astype(jnp.int32)
        rep_id = (group % N_REP).astype(jnp.int32)
        cols = cols_all[group]
        source = cols // BLOCKS_DEV * SECTION_BLOCKS + rep_id * BLOCKS_DEV + cols % BLOCKS_DEV
        target = section_id * SECTION_BLOCKS + rows_all[group]
        picked = node_blocks[source.astype(jnp.int32)].astype(jnp.float32)
        products = jnp.einsum('tij,tjf->tif', tiles[group].astype(jnp.float32), picked)
        live = (slot_ids < tile_counts[group]).astype(jnp.float32)
        total = total.at[target.astype(jnp.int32)].add(products * live[:, None, None])
        return (total, None)
    start = jnp.zeros((node_blocks.shape[0], BLOCK, F), jnp.float32)
    total, _ = lax.scan(visit, start, jnp.arange(GROUPS, dtype=jnp.int32))
    return total.reshape(-1, F)

def reference(node_features, tile_values, tile_rows, tile_cols, tile_counts, cheb_weights, bias, out_cotangent):
    first_sum = apply_operator(node_features, tile_values, tile_rows, tile_cols, tile_counts)
    first_hop = first_sum.astype(jnp.bfloat16)
    second_sum = apply_operator(first_hop, tile_values, tile_rows, tile_cols, tile_counts)
    second_hop = (2.0 * second_sum - node_features.astype(jnp.float32)).astype(jnp.bfloat16)
    stacked = jnp.concatenate([node_features, first_hop, second_hop], axis=1)
    pre_act = jnp.dot(stacked, cheb_weights, preferred_element_type=jnp.float32) + bias
    layer_out, backward = jax.vjp(smooth_gate, pre_act)
    pre_grad = backward(out_cotangent.astype(jnp.float32))[0].astype(jnp.bfloat16)
    weight_grads = jnp.dot(stacked.T, pre_grad, preferred_element_type=jnp.float32)
    return (layer_out.astype(jnp.bfloat16), weight_grads)
```

```python
import jax
import jax.numpy as jnp
from jax import lax
from jax.experimental import pallas as pl
from jax.experimental.pallas import tpu as pltpu
from jax.sharding import PartitionSpec as P

MESH = pl.DeviceIdType.MESH
N = 8
BLOCK = 128
F = 256
HALF = 128
TCAP = 16
BF16 = jnp.bfloat16
F32 = jnp.float32


def kernel(
    rows_ref, cols_ref, count_ref, x_ref, tiles_ref, w_ref, bias_ref, cot_ref,
    out_ref, grad_ref,
    *scratch,
):
    gathers_a, gathers_b = scratch[0:4], scratch[4:8]
    partials, arrivals = scratch[8:12], scratch[12:16]
    (adj, picked, hop1, hop2, grad_send, grad_recv, y_send, y_recv, z_all, y_all, rep_all,
     ring1_send, ring1_recv, ring2_send, ring2_recv, sum_send, sum_recv, red_send, red_recv) = scratch[16:]

    section = lax.axis_index("section")
    rep = lax.axis_index("rep")
    y = section // N
    z = section % N

    def ahead(pos, step):
        return lax.rem(pos + (step % N), N)

    def at_yz(yy, zz):
        return (yy * N + zz, rep)

    barrier = pltpu.get_barrier_semaphore()
    for d in range(1, N):
        for target in (at_yz(ahead(y, d), z), at_yz(y, ahead(z, d)), (section, ahead(rep, d))):
            pl.semaphore_signal(barrier, inc=1, device_id=target, device_id_type=MESH)
    pl.semaphore_wait(barrier, 3 * (N - 1))

    sends = []

    def remote(src, dst, send_sem, recv_sem, target):
        copy = pltpu.make_async_remote_copy(
            src_ref=src, dst_ref=dst, send_sem=send_sem, recv_sem=recv_sem,
            device_id=target, device_id_type=MESH,
        )
        copy.start()
        sends.append(copy)
        return copy

    orders = (
        (gathers_a, y, z, lambda u, v: at_yz(u, v)),
        (gathers_b, z, y, lambda u, v: at_yz(v, u)),
    )
    ring1, ring2 = {}, {}

    def ring1_put(stage, k):
        for o, (bufs, u, v, dev) in enumerate(orders):
            for way in (0, 1):
                if k > 3 + ((way + o + 1) % 2):
                    continue
                sign = 1 if way == 0 else -1
                piece = bufs[stage].at[u, ahead(v, -sign * (k - 1))]
                i = (stage, o, way, k - 1)
                ring1[i] = remote(piece, piece, ring1_send.at[i], ring1_recv.at[i], dev(u, ahead(v, sign)))

    def ring1_take(stage, k):
        for o in (0, 1):
            for way in (0, 1):
                if (stage, o, way, k - 1) in ring1:
                    ring1[stage, o, way, k - 1].wait_recv()

    def ring1_begin(stage, half):
        gathers_a[stage][y, z] = half[:64]
        gathers_b[stage][z, y] = half[64:]
        ring1_put(stage, 1)

    def ring1_step(stage, k):
        ring1_take(stage, k - 1)
        ring1_put(stage, k)

    def ring2_put(stage, k, o, way, sub):
        bufs, u, v, dev = orders[o]
        if k == 4 and sub != way:
            return
        sign = 1 if way == 0 else -1
        group = bufs[stage].at[ahead(u, -sign * (k - 1)), pl.ds(4 * sub, 4)]
        i = (stage, o, way, 2 * (k - 1) + sub)
        ring2[i] = remote(group, group, ring2_send.at[i], ring2_recv.at[i], dev(ahead(u, sign), v))

    def ring2_step(stage, k):
        for sub in (0, 1):
            for o in (0, 1):
                for way in (0, 1):
                    i = (stage, o, way, 2 * (k - 2) + sub)
                    if i in ring2:
                        ring2[i].wait_recv()
                    if k <= 4:
                        ring2_put(stage, k, o, way, sub)

    def ring2_begin(stage):
        ring2_step(stage, 1)

    def place_tiles():
        def one(t, _):
            tile = tiles_ref[t]
            row = jnp.where(t < count_ref[0], rows_ref[t], N)
            for b in range(N):
                adj[b * BLOCK:(b + 1) * BLOCK, pl.ds(pl.multiple_of(t * BLOCK, BLOCK), BLOCK)] = jnp.where(
                    row == b, tile, jnp.zeros_like(tile))
            return 0
        lax.fori_loop(0, TCAP, one, 0)

    sums = {}

    def multiply(stage):
        ga, gb = gathers_a[stage], gathers_b[stage]

        def pick(t, _):
            col = cols_ref[t]
            cy, cz = lax.div(col, N), lax.rem(col, N)
            at = pl.multiple_of(t * BLOCK, BLOCK)
            picked[pl.ds(at, 64), :] = ga[cy, cz]
            picked[pl.ds(at + 64, 64), :] = gb[cz, cy]
            return 0
        lax.fori_loop(0, TCAP, pick, 0)

        def rows(i, _):
            product = jnp.dot(adj[pl.ds(pl.multiple_of(i * 256, 256), 256), :], picked[...], preferred_element_type=F32)
            partials[stage][2 * i] = product[:BLOCK].astype(BF16)
            partials[stage][2 * i + 1] = product[BLOCK:].astype(BF16)
            return 0
        lax.fori_loop(0, N // 2, rows, 0)
        for d in range(1, N):
            to = ahead(rep, d)
            sums[stage, d] = remote(partials[stage].at[to], arrivals[stage].at[d - 1],
                                    sum_send.at[stage, d - 1], sum_recv.at[stage, d - 1], (section, to))

    def total(stage):
        for d in range(1, N):
            sums[stage, d].wait_recv()
        acc = partials[stage][rep].astype(F32)
        for d in range(1, N):
            acc += arrivals[stage][d - 1].astype(F32)
        return acc

    def first_total(c):
        half = total(c).astype(BF16)
        hop1[:, c * HALF:(c + 1) * HALF] = half
        ring1_begin(2 + c, half)

    def second_total(c):
        at = slice(c * HALF, (c + 1) * HALF)
        hop2[:, at] = (2.0 * total(2 + c) - x_ref[:, at].astype(F32)).astype(BF16)

    ring1_begin(0, x_ref[:, :HALF])
    ring1_begin(1, x_ref[:, HALF:])
    for k in (2, 3, 4):
        ring1_step(0, k)
        ring1_step(1, k)
    ring1_take(0, 4)
    ring2_begin(0)
    ring1_take(1, 4)
    place_tiles()
    ring2_step(0, 2)
    ring2_step(0, 3)
    ring2_step(0, 4)
    ring2_begin(1)
    ring2_step(0, 5)
    multiply(0)
    ring2_step(1, 2)
    first_total(0)
    ring2_step(1, 3)
    ring1_step(2, 2)
    ring1_step(2, 3)
    ring2_step(1, 4)
    ring1_step(2, 4)
    ring1_take(2, 4)
    ring2_begin(2)
    ring2_step(1, 5)
    multiply(1)
    ring2_step(2, 2)
    first_total(1)
    ring2_step(2, 3)
    ring1_step(3, 2)
    ring1_step(3, 3)
    ring2_step(2, 4)
    ring1_step(3, 4)
    ring1_take(3, 4)
    ring2_begin(3)
    ring2_step(2, 5)
    multiply(2)
    ring2_step(3, 2)
    second_total(0)
    ring2_step(3, 3)
    pre_act = jnp.dot(x_ref[...], w_ref[:F], preferred_element_type=F32)
    pre_act += jnp.dot(hop1[...], w_ref[F:2 * F], preferred_element_type=F32)
    pre_act += bias_ref[...]
    ring2_step(3, 4)
    ring2_step(3, 5)
    multiply(3)
    second_total(1)

    v = pre_act + jnp.dot(hop2[...], w_ref[2 * F:], preferred_element_type=F32)
    root = 0.7978845608028654
    th = jnp.tanh(root * (v + 0.044715 * (v * v * v)))
    cdf = 0.5 * (1.0 + th)
    out_ref[...] = (v * cdf).astype(BF16)
    slope = cdf + 0.5 * v * (1.0 - th * th) * (root * (1.0 + 3.0 * 0.044715 * (v * v)))
    pre_grad = (cot_ref[...].astype(F32) * slope).astype(BF16)
    for j, part in enumerate((x_ref, hop1, hop2)):
        local = lax.dot_general(part[...], pre_grad, (((0,), (0,)), ((), ())), preferred_element_type=F32)
        for i in range(8):
            row = j * 256 + i * 32
            grad_send[row // 96, row % 96:row % 96 + 32, :] = local[i * 32:(i + 1) * 32].astype(BF16)

    def exchange(base, source, target_ref, place, count=N):
        copies = []
        for d in range(1, N):
            src, dst, target = place(d)
            copies.append(remote(src, dst, red_send.at[base, d - 1], red_recv.at[base, d - 1], target))
        for copy in copies:
            copy.wait_recv()

    exchange(0, None, None, lambda d: (
        grad_send.at[ahead(rep, d)], grad_recv.at[d - 1], (section, ahead(rep, d))))
    acc = grad_send[rep].astype(F32)
    for d in range(1, N):
        acc += grad_recv[d - 1].astype(F32)
    for i in range(24):
        y_send[i // 3, i % 3] = acc[(i // 2) * 8:(i // 2 + 1) * 8, (i % 2) * 128:(i % 2 + 1) * 128]
    exchange(1, None, None, lambda d: (
        y_send.at[ahead(y, d)], y_recv.at[d - 1], at_yz(ahead(y, d), z)))
    acc = y_send[y]
    for d in range(1, N):
        acc += y_recv[d - 1]
    z_all[z] = acc
    exchange(2, None, None, lambda d: (z_all.at[z], z_all.at[z], at_yz(y, ahead(z, d))))
    acc = z_all[0]
    for i in range(1, N):
        acc += z_all[i]
    y_all[y] = acc
    exchange(3, None, None, lambda d: (y_all.at[y], y_all.at[y], at_yz(ahead(y, d), z)))
    whole = [y_all[i // 3, i % 3] for i in range(24)]
    rep_all[rep] = jnp.concatenate(
        [jnp.concatenate([whole[2 * i], whole[2 * i + 1]], axis=1) for i in range(12)], axis=0).astype(BF16)
    exchange(4, None, None, lambda d: (rep_all.at[rep], rep_all.at[rep], (section, ahead(rep, d))))
    for i in range(N):
        grad_ref[i * 96:(i + 1) * 96, :] = rep_all[i].astype(F32)

    for copy in sends:
        copy.wait_send()


def body(node_features, tile_values, tile_rows, tile_cols, tile_counts, cheb_weights, bias, out_cotangent):
    vmem = pl.BlockSpec(memory_space=pltpu.VMEM)
    smem = pl.BlockSpec(memory_space=pltpu.SMEM)
    dma = pltpu.SemaphoreType.DMA
    scratch = (
        [pltpu.VMEM((N, N, 64, HALF), BF16)] * 8
        + [pltpu.VMEM((N, BLOCK, HALF), BF16)] * 4
        + [pltpu.VMEM((N - 1, BLOCK, HALF), BF16)] * 4
        + [
            pltpu.VMEM((N * BLOCK, TCAP * BLOCK), BF16),
            pltpu.VMEM((TCAP * BLOCK, HALF), BF16),
            pltpu.VMEM((BLOCK, F), BF16),
            pltpu.VMEM((BLOCK, F), BF16),
            pltpu.VMEM((N, 96, F), BF16),
            pltpu.VMEM((N - 1, 96, F), BF16),
            pltpu.VMEM((N, 3, 8, 128), F32),
            pltpu.VMEM((N - 1, 3, 8, 128), F32),
            pltpu.VMEM((N, 3, 8, 128), F32),
            pltpu.VMEM((N, 3, 8, 128), F32),
            pltpu.VMEM((N, 96, F), BF16),
            dma((4, 2, 2, 4)), dma((4, 2, 2, 4)),
            dma((4, 2, 2, 8)), dma((4, 2, 2, 8)),
            dma((4, N - 1)), dma((4, N - 1)),
            dma((5, N - 1)), dma((5, N - 1)),
        ]
    )
    return pl.pallas_call(
        kernel,
        out_shape=(
            jax.ShapeDtypeStruct((BLOCK, F), BF16),
            jax.ShapeDtypeStruct((3 * F, F), F32),
        ),
        in_specs=[smem] * 3 + [vmem] * 5,
        out_specs=(vmem, vmem),
        scratch_shapes=scratch,
        compiler_params=pltpu.CompilerParams(
            collective_id=0, has_side_effects=True, vmem_limit_bytes=40 * 1024 * 1024),
        cost_estimate=pl.CostEstimate(flops=2 * 10**9, bytes_accessed=4 * 10**6, transcendentals=BLOCK * F),
    )(tile_rows, tile_cols, tile_counts, node_features, tile_values, cheb_weights, bias.reshape(1, F), out_cotangent)


def solution(mesh):
    return jax.shard_map(
        body,
        mesh=mesh,
        in_specs=(
            P(("section", "rep"), None),
            P(("section", "rep"), None, None),
            P(("section", "rep")),
            P(("section", "rep")),
            P(("section", "rep")),
            P(),
            P(),
            P(("section", "rep"), None),
        ),
        out_specs=(P(("section", "rep"), None), P()),
        check_vma=False,
    )
```

```python
import jax
import jax.numpy as jnp
from jax import lax
from jax.experimental import pallas as pl
from jax.experimental.pallas import tpu as pltpu
from jax.sharding import PartitionSpec as P

MESH = pl.DeviceIdType.MESH
N = 8
BLOCK = 128
F = 256
HALF = 128
TCAP = 16
BF16 = jnp.bfloat16
F32 = jnp.float32


RANK = (0, 1, 3, 5, 7, 6, 4, 2)
GROUPS = ((0, 1), (1, 3), (3, 5), (5, 8))
CHIPS = 4


def kernel(
    rows_ref, cols_ref, count_ref, x_hbm, tiles_hbm, w_hbm, bias_hbm, cot_hbm,
    out_ref, grad_ref,
    *scratch,
):
    gathers_a, gathers_b = scratch[0:4], scratch[4:8]
    partials, arrivals, own_sums = scratch[8:12], scratch[12:16], scratch[16:20]
    (x_ref, tiles_ref, w_ref, bias_ref, cot_ref, load_sem,
     adj, picked, hop1, hop2,
     grad_own, core_send, core_recv, x_own, x_send, x_recv, y_send, y_recv, z_all, y_all, rep_all,
     line_send, line_recv, ring_send, ring_recv, sum_send, sum_recv, red_send, red_recv) = scratch[20:]

    section = lax.axis_index("section")
    rep = lax.axis_index("rep")
    y = section // N
    z = section % N
    chip = rep // 2
    core = rep % 2
    other = 1 - core

    def ahead(pos, step):
        return lax.rem(pos + (step % N), N)

    def chip_ahead(step):
        return lax.rem(chip + step % CHIPS, CHIPS)

    def at_yz(yy, zz):
        return (yy * N + zz, rep)

    loads = [
        pltpu.make_async_copy(src, dst, load_sem.at[i])
        for i, (src, dst) in enumerate((
            (x_hbm, x_ref), (tiles_hbm, tiles_ref), (w_hbm, w_ref), (bias_hbm, bias_ref), (cot_hbm, cot_ref)))
    ]
    for load in loads:
        load.start()

    barrier = pltpu.get_barrier_semaphore()
    for d in range(1, N):
        for target in (at_yz(ahead(y, d), z), at_yz(y, ahead(z, d)), (section, ahead(rep, d))):
            pl.semaphore_signal(barrier, inc=1, device_id=target, device_id_type=MESH)

    loads[1].wait()

    def place(t, _):
        tile = tiles_ref[t]
        row = jnp.where(t < count_ref[0], rows_ref[t], N)
        for b in range(N):
            adj[b * BLOCK:(b + 1) * BLOCK, pl.ds(pl.multiple_of(t * BLOCK, BLOCK), BLOCK)] = jnp.where(
                row == b, tile, jnp.zeros_like(tile))
        return 0
    lax.fori_loop(0, TCAP, place, 0)
    for i in (0, 2, 3, 4):
        loads[i].wait()

    pl.semaphore_wait(barrier, 3 * (N - 1))

    sends = []

    def describe(src, dst, send_sem, recv_sem, target):
        return pltpu.make_async_remote_copy(
            src_ref=src, dst_ref=dst, send_sem=send_sem, recv_sem=recv_sem,
            device_id=target, device_id_type=MESH,
        )

    def remote(*args):
        copy = describe(*args)
        copy.start()
        sends.append(copy)
        return copy

    def drain():
        for copy in sends:
            copy.wait_send()
        sends.clear()

    orders = (
        (gathers_a, y, z, lambda u, v: at_yz(u, v)),
        (gathers_b, z, y, lambda u, v: at_yz(v, u)),
    )
    line, ring = {}, {}

    def ring_put(stage, g, k, o, way):
        bufs, u, v, dev = orders[o]
        first, last = GROUPS[g]
        if k == 4:
            first, last = (first, min(last, 4)) if way == 0 else (max(first, 4), last)
            if first >= last:
                return
        sign = 1 if way == 0 else -1
        group = bufs[stage].at[ahead(u, -sign * (k - 1)), pl.ds(first, last - first)]
        i = (stage, o, way, (k - 1) * 4 + g)
        ring[stage, g, k, o, way] = remote(group, group, ring_send.at[i], ring_recv.at[i], dev(ahead(u, sign), v))

    def ring_step(stage, g, k):
        for o in (0, 1):
            if k == 1:
                for j in range(*GROUPS[g]):
                    if j:
                        line[stage, o, j].wait_recv()
            for way in (0, 1):
                if (stage, g, k - 1, o, way) in ring:
                    ring[stage, g, k - 1, o, way].wait_recv()
                if k <= 4:
                    ring_put(stage, g, k, o, way)

    def gather_begin(stage, half):
        gathers_a[stage][y, 0] = half[:64]
        gathers_b[stage][z, 0] = half[64:]
        for d in (1, 7, 2, 6, 3, 5, 4):
            for o, (bufs, u, v, dev) in enumerate(orders):
                if d == 2:
                    for way in (0, 1):
                        ring_put(stage, 0, 1, o, way)
                j = RANK[-d % N]
                i = (stage, o, d - 1)
                line[stage, o, j] = remote(
                    bufs[stage].at[u, 0], bufs[stage].at[u, j], line_send.at[i], line_recv.at[i], dev(u, ahead(v, d)))

    def gather_round(stage, n):
        for g in range(4):
            k = n + 1 if g == 0 else n
            if k <= 5:
                ring_step(stage, g, k)

    def multiply(stage):
        ga, gb = gathers_a[stage], gathers_b[stage]

        def rank(d):
            d = lax.rem(d + N, N)
            return jnp.where(d <= 4, jnp.maximum(2 * d - 1, 0), 2 * (N - d))

        def pick(t, _):
            col = cols_ref[t]
            cy, cz = lax.div(col, N), lax.rem(col, N)
            at = pl.multiple_of(t * BLOCK, BLOCK)
            picked[pl.ds(at, 64), :] = ga[cy, rank(cz - z)]
            picked[pl.ds(at + 64, 64), :] = gb[cz, rank(cy - y)]
            return 0
        lax.fori_loop(0, TCAP, pick, 0, unroll=4)

        for i in (2, 1, 3, 0):
            to = chip_ahead(i)
            product = jnp.dot(
                adj[pl.ds(pl.multiple_of(to * 256, 256), 256), :], picked[...], preferred_element_type=F32)
            partials[stage][i, 0] = product[:BLOCK].astype(BF16)
            partials[stage][i, 1] = product[BLOCK:].astype(BF16)
            if i:
                for c in (0, 1):
                    remote(partials[stage].at[i, c], arrivals[stage].at[i, core],
                           sum_send.at[stage, i, c], sum_recv.at[stage, i, core], (section, to * 2 + c))
            else:
                own_sums[stage][...] = jnp.where(core == 0, product[:BLOCK], product[BLOCK:])
                remote(partials[stage].at[0, other], arrivals[stage].at[0, 0],
                       sum_send.at[stage, 0, 0], sum_recv.at[stage, 0, 0], (section, chip * 2 + other))

    def total(stage):
        acc = own_sums[stage][...]
        for i, c in ((0, 0), (1, 0), (1, 1), (3, 0), (3, 1), (2, 0), (2, 1)):
            describe(partials[stage].at[i, c], arrivals[stage].at[i, c], sum_send.at[stage, i, c],
                     sum_recv.at[stage, i, c], (section, chip * 2 + other)).wait_recv()
            acc += arrivals[stage][i, c].astype(F32)
        return acc

    def first_total(c):
        half = total(c).astype(BF16)
        hop1[:, c * HALF:(c + 1) * HALF] = half
        gather_begin(2 + c, half)

    def second_total(c):
        at = slice(c * HALF, (c + 1) * HALF)
        hop2[:, at] = (2.0 * total(2 + c) - x_ref[:, at].astype(F32)).astype(BF16)

    gather_begin(0, x_ref[:, :HALF])
    gather_round(0, 1)
    gather_begin(1, x_ref[:, HALF:])
    gather_round(0, 2)
    gather_round(1, 1)
    gather_round(0, 3)
    gather_round(0, 4)
    gather_round(1, 2)
    gather_round(0, 5)
    multiply(0)
    gather_round(1, 3)
    first_total(0)
    gather_round(1, 4)
    gather_round(2, 1)
    gather_round(1, 5)
    multiply(1)
    gather_round(2, 2)
    gather_round(2, 3)
    first_total(1)
    gather_round(2, 4)
    gather_round(3, 1)
    gather_round(2, 5)
    multiply(2)
    gather_round(3, 2)
    gather_round(3, 3)
    second_total(0)
    pre_act = jnp.dot(x_ref[...], w_ref[:F], preferred_element_type=F32)
    pre_act += jnp.dot(hop1[...], w_ref[F:2 * F], preferred_element_type=F32)
    pre_act += bias_ref[...]
    gather_round(3, 4)
    gather_round(3, 5)
    multiply(3)
    second_total(1)

    v = pre_act + jnp.dot(hop2[...], w_ref[2 * F:], preferred_element_type=F32)
    root = 0.7978845608028654
    th = jnp.tanh(root * (v + 0.044715 * (v * v * v)))
    cdf = 0.5 * (1.0 + th)
    slope = cdf + 0.5 * v * (1.0 - th * th) * (root * (1.0 + 3.0 * 0.044715 * (v * v)))
    pre_grad = (cot_ref[...].astype(F32) * slope).astype(BF16)
    for j, part in enumerate((x_ref, hop1, hop2)):
        local = lax.dot_general(part[...], pre_grad, (((0,), (0,)), ((), ())), preferred_element_type=F32)
        for i in range(8):
            row = j * 256 + i * 32
            q, at = row // 96, row % 96
            value = local[i * 32:(i + 1) * 32]
            grad_own[q // 4, q % 4, at:at + 32, :] = value
            core_send[q // 4, q % 4, at:at + 32, :] = value.astype(BF16)

    def start(step, d, src, dst, target):
        return remote(src, dst, red_send.at[step, d], red_recv.at[step, d], target)

    sibling = (section, chip * 2 + other)
    swap = start(0, 0, core_send.at[other], core_recv, sibling)
    out_ref[...] = (v * cdf).astype(BF16)
    swap.wait_recv()
    for i in range(CHIPS):
        value = grad_own[core, i] + core_recv[i].astype(F32)
        x_own[i] = value
        x_send[i] = value.astype(BF16)
    copies = [
        start(1, i, x_send.at[chip_ahead(i)], x_recv.at[i - 1], (section, chip_ahead(i) * 2 + core)) for i in (2, 1, 3)]
    acc = x_own[chip]
    for i, copy in zip((2, 1, 3), copies):
        copy.wait_recv()
        acc += x_recv[i - 1].astype(F32)
    for i in range(24):
        y_send[i // 3, i % 3] = acc[(i // 2) * 8:(i // 2 + 1) * 8, (i % 2) * 128:(i % 2 + 1) * 128]
    far = (4, 3, 5, 2, 6, 1, 7)
    copies = [start(2, d, y_send.at[ahead(y, d)], y_recv.at[d - 1], at_yz(ahead(y, d), z)) for d in far]
    drain_later = sends[:-len(far)]
    del sends[:-len(far)]
    for copy in drain_later:
        copy.wait_send()
    acc = y_send[y]
    for copy in copies:
        copy.wait_recv()
    for d in range(1, N):
        acc += y_recv[d - 1]
    z_all[z] = acc
    copies = [start(3, d, z_all.at[z], z_all.at[z], at_yz(y, ahead(z, d))) for d in far]
    for copy in copies:
        copy.wait_recv()
    acc = z_all[0]
    for i in range(1, N):
        acc += z_all[i]
    y_all[y] = jnp.concatenate([acc[0], acc[1], acc[2], jnp.zeros_like(acc[0])], axis=0).astype(BF16)
    copies = [start(4, d, y_all.at[y], y_all.at[y], at_yz(ahead(y, d), z)) for d in far]
    for copy in copies:
        copy.wait_recv()
    whole = [y_all[i // 3][(i % 3) * 8:(i % 3 + 1) * 8].astype(F32) for i in range(24)]
    rep_all[core, chip] = jnp.concatenate(
        [jnp.concatenate([whole[2 * i], whole[2 * i + 1]], axis=1) for i in range(12)], axis=0).astype(BF16)
    copies = [
        start(5, i, rep_all.at[core, chip], rep_all.at[core, chip], (section, chip_ahead(i) * 2 + core)) for i in (2, 1, 3)]
    across = [start(6, 0, rep_all.at[core, chip], rep_all.at[core, chip], sibling)]
    for i, copy in ((1, copies[1]), (3, copies[2]), (2, copies[0])):
        copy.wait_recv()
        came = rep_all.at[core, chip_ahead(-i)]
        across.append(start(6, i, came, came, sibling))
    for copy in across:
        copy.wait_recv()
    for i in range(N):
        grad_ref[i * 96:(i + 1) * 96, :] = rep_all[i // 4, i % 4]

    drain()


def body(node_features, tile_values, tile_rows, tile_cols, tile_counts, cheb_weights, bias, out_cotangent):
    vmem = pl.BlockSpec(memory_space=pltpu.VMEM)
    smem = pl.BlockSpec(memory_space=pltpu.SMEM)
    anywhere = pl.BlockSpec(memory_space=pl.ANY)
    dma = pltpu.SemaphoreType.DMA
    scratch = (
        [pltpu.VMEM((N, N, 64, HALF), BF16)] * 8
        + [pltpu.VMEM((CHIPS, 2, BLOCK, HALF), BF16)] * 8
        + [pltpu.VMEM((BLOCK, HALF), F32)] * 4
        + [
            pltpu.VMEM((BLOCK, F), BF16),
            pltpu.VMEM((TCAP, BLOCK, BLOCK), BF16),
            pltpu.VMEM((3 * F, F), BF16),
            pltpu.VMEM((1, F), F32),
            pltpu.VMEM((BLOCK, F), BF16),
            dma((5,)),
            pltpu.VMEM((N * BLOCK, TCAP * BLOCK), BF16),
            pltpu.VMEM((TCAP * BLOCK, HALF), BF16),
            pltpu.VMEM((BLOCK, F), BF16),
            pltpu.VMEM((BLOCK, F), BF16),
            pltpu.VMEM((2, CHIPS, 96, F), F32),
            pltpu.VMEM((2, CHIPS, 96, F), BF16),
            pltpu.VMEM((CHIPS, 96, F), BF16),
            pltpu.VMEM((CHIPS, 96, F), F32),
            pltpu.VMEM((CHIPS, 96, F), BF16),
            pltpu.VMEM((CHIPS - 1, 96, F), BF16),
            pltpu.VMEM((N, 3, 8, 128), F32),
            pltpu.VMEM((N - 1, 3, 8, 128), F32),
            pltpu.VMEM((N, 3, 8, 128), F32),
            pltpu.VMEM((N, 32, 128), BF16),
            pltpu.VMEM((2, CHIPS, 96, F), BF16),
            dma((4, 2, N - 1)), dma((4, 2, N - 1)),
            dma((4, 2, 2, 16)), dma((4, 2, 2, 16)),
            dma((4, CHIPS, 2)), dma((4, CHIPS, 2)),
            dma((7, N)), dma((7, N)),
        ]
    )
    layer_out, grads = pl.pallas_call(
        kernel,
        out_shape=(
            jax.ShapeDtypeStruct((BLOCK, F), BF16),
            jax.ShapeDtypeStruct((3 * F, F), BF16),
        ),
        in_specs=[smem] * 3 + [anywhere] * 5,
        out_specs=(vmem, vmem),
        scratch_shapes=scratch,
        compiler_params=pltpu.CompilerParams(
            collective_id=0, has_side_effects=True, vmem_limit_bytes=56 * 1024 * 1024),
        cost_estimate=pl.CostEstimate(flops=2 * 10**9, bytes_accessed=4 * 10**6, transcendentals=BLOCK * F),
    )(tile_rows, tile_cols, tile_counts, node_features, tile_values, cheb_weights, bias.reshape(1, F), out_cotangent)
    return layer_out, grads.astype(F32)


def solution(mesh):
    return jax.shard_map(
        body,
        mesh=mesh,
        in_specs=(
            P(("section", "rep"), None),
            P(("section", "rep"), None, None),
            P(("section", "rep")),
            P(("section", "rep")),
            P(("section", "rep")),
            P(),
            P(),
            P(("section", "rep"), None),
        ),
        out_specs=(P(("section", "rep"), None), P()),
        check_vma=False,
    )
```

```python
import jax
import jax.numpy as jnp
from jax import lax
from jax.experimental import pallas as pl
from jax.experimental.pallas import tpu as pltpu
from jax.sharding import PartitionSpec as P

MESH = pl.DeviceIdType.MESH
N = 8
BLOCK = 128
F = 256
HALF = 128
TCAP = 16
BF16 = jnp.bfloat16
F32 = jnp.float32


RANK = (0, 1, 3, 5, 7, 6, 4, 2)
GROUPS = ((0, 1), (1, 3), (3, 5), (5, 7), (7, 8))
LINE = 0
ORDER = (
    (0, 1, LINE), (0, 0, 1), (0, 2, LINE), (1, 1, LINE), (1, 0, 1), (1, 2, LINE), (0, 0, 2), (0, 3, LINE), (0, 1, 1), (1, 0, 2),
    (0, 2, 1), (1, 3, LINE), (1, 1, 1), (1, 2, 1), (0, 0, 3), (0, 4, LINE), (0, 1, 2), (0, 3, 1), (1, 0, 3), (1, 4, LINE),
    (0, 2, 2), (0, 4, 1), (1, 3, 1), (1, 1, 2), (1, 2, 2), (1, 4, 1), (0, 3, 2), (0, 1, 3), (0, 4, 2), (0, 2, 3),
    (1, 3, 2), (1, 1, 3), (1, 4, 2), (1, 2, 3), (0, 3, 3), (0, 4, 3), (1, 3, 3), (1, 4, 3),
)
CHIPS = 4


def kernel(
    rows_ref, cols_ref, count_ref, x_hbm, tiles_hbm, w_hbm, bias_hbm, cot_hbm,
    out_ref, grad_ref,
    *scratch,
):
    gathers_a, gathers_b = scratch[0:4], scratch[4:8]
    partials, arrivals, own_sums = scratch[8:12], scratch[12:16], scratch[16:20]
    (x_ref, tiles_ref, w_ref, bias_ref, cot_ref, load_sem,
     adj, picked, hop1, hop2,
     grad_own, core_send, core_recv, x_own, x_send, x_recv, y_send, y_recv, z_all, y_all, rep_all,
     line_send, line_recv, ring_send, ring_recv, sum_send, sum_recv, red_send, red_recv) = scratch[20:]

    section = lax.axis_index("section")
    rep = lax.axis_index("rep")
    y = section // N
    z = section % N
    chip = rep // 2
    core = rep % 2
    other = 1 - core

    def ahead(pos, step):
        return lax.rem(pos + (step % N), N)

    def chip_ahead(step):
        return lax.rem(chip + step % CHIPS, CHIPS)

    def at_yz(yy, zz):
        return (yy * N + zz, rep)

    loads = [
        pltpu.make_async_copy(src, dst, load_sem.at[i])
        for i, (src, dst) in enumerate((
            (x_hbm, x_ref), (tiles_hbm, tiles_ref), (w_hbm, w_ref), (bias_hbm, bias_ref), (cot_hbm, cot_ref)))
    ]
    for load in loads:
        load.start()

    barrier = pltpu.get_barrier_semaphore()
    for d in range(1, N):
        for target in (at_yz(ahead(y, d), z), at_yz(y, ahead(z, d)), (section, ahead(rep, d))):
            pl.semaphore_signal(barrier, inc=1, device_id=target, device_id_type=MESH)

    loads[1].wait()

    def place(t, _):
        tile = tiles_ref[t]
        row = jnp.where(t < count_ref[0], rows_ref[t], N)
        for b in range(N):
            adj[b * BLOCK:(b + 1) * BLOCK, pl.ds(pl.multiple_of(t * BLOCK, BLOCK), BLOCK)] = jnp.where(
                row == b, tile, jnp.zeros_like(tile))
        return 0
    lax.fori_loop(0, TCAP, place, 0)
    for i in (0, 2, 3, 4):
        loads[i].wait()

    pl.semaphore_wait(barrier, 3 * (N - 1))

    def describe(src, dst, send_sem, recv_sem, target):
        return pltpu.make_async_remote_copy(
            src_ref=src, dst_ref=dst, send_sem=send_sem, recv_sem=recv_sem,
            device_id=target, device_id_type=MESH,
        )

    def remote(*args):
        describe(*args).start()

    sibling = (section, chip * 2 + other)

    def arrived(ref, sem):
        describe(ref, ref, sem, sem, sibling).wait_recv()

    def departed(ref, sem):
        describe(ref, ref, sem, sem, sibling).wait_send()

    orders = (
        (gathers_a, y, z, lambda u, v: at_yz(u, v)),
        (gathers_b, z, y, lambda u, v: at_yz(v, u)),
    )

    def line_put(stage, o, way, dist, hops):
        bufs, u, v, dev = orders[o]
        sign = 1 if way == 0 else -1
        remote(bufs[stage].at[u, RANK[-sign * (dist - hops) % N]], bufs[stage].at[u, RANK[-sign * dist % N]],
               line_send.at[stage, o], line_recv.at[stage, dist - 1], dev(u, ahead(v, sign * hops)))

    def ring_put(stage, g, k):
        for o, (bufs, u, v, dev) in enumerate(orders):
            for way, sign in ((0, 1), (1, -1)):
                first, last = GROUPS[g]
                if k == 4:
                    first, last = (first, min(last, 4)) if way == 0 else (max(first, 4), last)
                    if first >= last:
                        continue
                group = bufs[stage].at[ahead(u, -sign * (k - 1)), pl.ds(first, last - first)]
                remote(group, group, ring_send.at[stage, o], ring_recv.at[stage, g * 4 + k - 1], dev(ahead(u, sign), v))

    def ring_take(stage, g, k):
        first, last = GROUPS[g]
        arrived(gathers_a[stage].at[pl.ds(0, 2 if k == 4 else 4), pl.ds(first, last - first)],
                ring_recv.at[stage, g * 4 + k - 1])

    def gather_begin(stage, half):
        gathers_a[stage][y, 0] = half[:64]
        gathers_b[stage][z, 0] = half[64:]
        for dist in (1, 2):
            for o in (0, 1):
                for way in (0, 1):
                    line_put(stage, o, way, dist, dist)
        ring_put(stage, 0, 1)

    def gather_pair(base):
        for c, g, k in ORDER:
            stage = base + c
            if k == LINE:
                arrived(gathers_a[stage].at[pl.ds(0, 2 if g == 4 else 4), 0], line_recv.at[stage, g - 1])
                for o in (0, 1):
                    for way in (0, 1):
                        if g == 2 or (g == 3 and way == o):
                            line_put(stage, o, way, g + 1, 1)
                ring_put(stage, g, 1)
            else:
                ring_take(stage, g, k)
                ring_put(stage, g, k + 1)

    def gather_end(stage):
        for g in range(5):
            ring_take(stage, g, 4)

    def gather_departed(stage):
        for o, bufs in ((0, gathers_a), (1, gathers_b)):
            departed(bufs[stage].at[0, pl.ds(0, N - 1)], line_send.at[stage, o])
            departed(bufs[stage].at[pl.ds(0, N - 1)], ring_send.at[stage, o])
        departed(partials[stage].at[pl.ds(1, 3)], sum_send.at[stage, 1])
        departed(partials[stage].at[0, 0], sum_send.at[stage, 0])

    def multiply(stage):
        ga, gb = gathers_a[stage], gathers_b[stage]

        def rank(d):
            d = lax.rem(d + N, N)
            return jnp.where(d <= 4, jnp.maximum(2 * d - 1, 0), 2 * (N - d))

        def pick(t, _):
            col = cols_ref[t]
            cy, cz = lax.div(col, N), lax.rem(col, N)
            at = pl.multiple_of(t * BLOCK, BLOCK)
            picked[pl.ds(at, 64), :] = ga[cy, rank(cz - z)]
            picked[pl.ds(at + 64, 64), :] = gb[cz, rank(cy - y)]
            return 0
        lax.fori_loop(0, TCAP, pick, 0, unroll=4)

        for i in (2, 1, 3, 0):
            to = chip_ahead(i)
            product = jnp.dot(
                adj[pl.ds(pl.multiple_of(to * 256, 256), 256), :], picked[...], preferred_element_type=F32)
            partials[stage][i, 0] = product[:BLOCK].astype(BF16)
            partials[stage][i, 1] = product[BLOCK:].astype(BF16)
            if i:
                for c in (0, 1):
                    remote(partials[stage].at[i, c], arrivals[stage].at[i, core],
                           sum_send.at[stage, 1], sum_recv.at[stage, 1], (section, to * 2 + c))
            else:
                own_sums[stage][...] = jnp.where(core == 0, product[:BLOCK], product[BLOCK:])
                remote(partials[stage].at[0, other], arrivals[stage].at[0, 0],
                       sum_send.at[stage, 0], sum_recv.at[stage, 0], sibling)

    def total(stage):
        arrived(arrivals[stage].at[0, 0], sum_recv.at[stage, 0])
        acc = own_sums[stage][...] + arrivals[stage][0, 0].astype(F32)
        arrived(arrivals[stage].at[pl.ds(1, 3)], sum_recv.at[stage, 1])
        for i in (1, 2, 3):
            for c in (0, 1):
                acc += arrivals[stage][i, c].astype(F32)
        return acc

    def first_total(c):
        half = total(c).astype(BF16)
        hop1[:, c * HALF:(c + 1) * HALF] = half
        gather_begin(2 + c, half)

    def second_total(c):
        at = slice(c * HALF, (c + 1) * HALF)
        hop2[:, at] = (2.0 * total(2 + c) - x_ref[:, at].astype(F32)).astype(BF16)

    gather_begin(0, x_ref[:, :HALF])
    gather_begin(1, x_ref[:, HALF:])
    gather_pair(0)
    gather_end(0)
    multiply(0)
    gather_end(1)
    multiply(1)
    first_total(0)
    first_total(1)
    gather_pair(2)
    gather_end(2)
    multiply(2)
    gather_end(3)
    multiply(3)
    pre_act = jnp.dot(x_ref[...], w_ref[:F], preferred_element_type=F32)
    pre_act += jnp.dot(hop1[...], w_ref[F:2 * F], preferred_element_type=F32)
    pre_act += bias_ref[...]
    second_total(0)
    second_total(1)

    v = pre_act + jnp.dot(hop2[...], w_ref[2 * F:], preferred_element_type=F32)
    root = 0.7978845608028654
    th = jnp.tanh(root * (v + 0.044715 * (v * v * v)))
    cdf = 0.5 * (1.0 + th)
    slope = cdf + 0.5 * v * (1.0 - th * th) * (root * (1.0 + 3.0 * 0.044715 * (v * v)))
    pre_grad = (cot_ref[...].astype(F32) * slope).astype(BF16)
    for j, part in enumerate((x_ref, hop1, hop2)):
        local = lax.dot_general(part[...], pre_grad, (((0,), (0,)), ((), ())), preferred_element_type=F32)
        for i in range(8):
            row = j * 256 + i * 32
            q, at = row // 96, row % 96
            value = local[i * 32:(i + 1) * 32]
            grad_own[q // 4, q % 4, at:at + 32, :] = value
            core_send[q // 4, q % 4, at:at + 32, :] = value.astype(BF16)

    def start(send, recv, src, dst, target):
        remote(src, dst, red_send.at[send], red_recv.at[recv], target)

    start(0, 0, core_send.at[other], core_recv, sibling)
    out_ref[...] = (v * cdf).astype(BF16)
    arrived(core_recv, red_recv.at[0])
    for i in range(CHIPS):
        value = grad_own[core, i] + core_recv[i].astype(F32)
        x_own[i] = value
        x_send[i] = value.astype(BF16)
    for i in (2, 1, 3):
        start(1, 1, x_send.at[chip_ahead(i)], x_recv.at[i - 1], (section, chip_ahead(i) * 2 + core))
    departed(core_send.at[0], red_send.at[0])
    gather_departed(0)
    gather_departed(1)
    arrived(x_recv, red_recv.at[1])
    acc = x_own[chip]
    for i in range(CHIPS - 1):
        acc += x_recv[i].astype(F32)
    for i in range(24):
        y_send[i // 3, i % 3] = acc[(i // 2) * 8:(i // 2 + 1) * 8, (i % 2) * 128:(i % 2 + 1) * 128]
    far = (4, 3, 5, 2, 6, 1, 7)
    for d in far:
        start(2, 2, y_send.at[ahead(y, d)], y_recv.at[d - 1], at_yz(ahead(y, d), z))
    departed(x_send.at[pl.ds(0, CHIPS - 1)], red_send.at[1])
    gather_departed(2)
    gather_departed(3)
    acc = y_send[y]
    arrived(y_recv, red_recv.at[2])
    for d in range(1, N):
        acc += y_recv[d - 1]
    z_all[z] = acc
    for d in far:
        start(3, 3, z_all.at[z], z_all.at[z], at_yz(y, ahead(z, d)))
    arrived(z_all.at[pl.ds(0, N - 1)], red_recv.at[3])
    acc = z_all[0]
    for i in range(1, N):
        acc += z_all[i]
    y_all[y] = jnp.concatenate([acc[0], acc[1], acc[2], jnp.zeros_like(acc[0])], axis=0).astype(BF16)
    for d in far:
        start(4, 4, y_all.at[y], y_all.at[y], at_yz(ahead(y, d), z))
    departed(y_recv, red_send.at[2])
    departed(z_all.at[pl.ds(0, N - 1)], red_send.at[3])
    arrived(y_all.at[pl.ds(0, N - 1)], red_recv.at[4])
    whole = [y_all[i // 3][(i % 3) * 8:(i % 3 + 1) * 8].astype(F32) for i in range(24)]
    rep_all[core, chip] = jnp.concatenate(
        [jnp.concatenate([whole[2 * i], whole[2 * i + 1]], axis=1) for i in range(12)], axis=0).astype(BF16)
    mine = rep_all.at[core, chip]
    for i in (2, 1, 3):
        start(5, 5 + i, mine, mine, (section, chip_ahead(i) * 2 + core))
    start(6, 5, mine, mine, sibling)
    departed(y_all.at[pl.ds(0, N - 1)], red_send.at[4])
    for i in (1, 3, 2):
        came = rep_all.at[core, chip_ahead(-i)]
        arrived(came, red_recv.at[5 + i])
        start(6, 5, came, came, sibling)
    arrived(rep_all.at[other], red_recv.at[5])
    for i in range(N):
        grad_ref[i * 96:(i + 1) * 96, :] = rep_all[i // 4, i % 4].astype(F32)
    departed(rep_all.at[0, pl.ds(0, CHIPS - 1)], red_send.at[5])
    departed(rep_all.at[0], red_send.at[6])


def body(node_features, tile_values, tile_rows, tile_cols, tile_counts, cheb_weights, bias, out_cotangent):
    vmem = pl.BlockSpec(memory_space=pltpu.VMEM)
    smem = pl.BlockSpec(memory_space=pltpu.SMEM)
    anywhere = pl.BlockSpec(memory_space=pl.ANY)
    dma = pltpu.SemaphoreType.DMA
    scratch = (
        [pltpu.VMEM((N, N, 64, HALF), BF16)] * 8
        + [pltpu.VMEM((CHIPS, 2, BLOCK, HALF), BF16)] * 8
        + [pltpu.VMEM((BLOCK, HALF), F32)] * 4
        + [
            pltpu.VMEM((BLOCK, F), BF16),
            pltpu.VMEM((TCAP, BLOCK, BLOCK), BF16),
            pltpu.VMEM((3 * F, F), BF16),
            pltpu.VMEM((1, F), F32),
            pltpu.VMEM((BLOCK, F), BF16),
            dma((5,)),
            pltpu.VMEM((N * BLOCK, TCAP * BLOCK), BF16),
            pltpu.VMEM((TCAP * BLOCK, HALF), BF16),
            pltpu.VMEM((BLOCK, F), BF16),
            pltpu.VMEM((BLOCK, F), BF16),
            pltpu.VMEM((2, CHIPS, 96, F), F32),
            pltpu.VMEM((2, CHIPS, 96, F), BF16),
            pltpu.VMEM((CHIPS, 96, F), BF16),
            pltpu.VMEM((CHIPS, 96, F), F32),
            pltpu.VMEM((CHIPS, 96, F), BF16),
            pltpu.VMEM((CHIPS - 1, 96, F), BF16),
            pltpu.VMEM((N, 3, 8, 128), F32),
            pltpu.VMEM((N - 1, 3, 8, 128), F32),
            pltpu.VMEM((N, 3, 8, 128), F32),
            pltpu.VMEM((N, 32, 128), BF16),
            pltpu.VMEM((2, CHIPS, 96, F), BF16),
            dma((4, 2)), dma((4, 4)),
            dma((4, 2)), dma((4, 20)),
            dma((4, 2)), dma((4, 2)),
            dma((7,)), dma((9,)),
        ]
    )
    return pl.pallas_call(
        kernel,
        out_shape=(
            jax.ShapeDtypeStruct((BLOCK, F), BF16),
            jax.ShapeDtypeStruct((3 * F, F), F32),
        ),
        in_specs=[smem] * 3 + [anywhere] * 5,
        out_specs=(vmem, vmem),
        scratch_shapes=scratch,
        compiler_params=pltpu.CompilerParams(
            collective_id=0, has_side_effects=True, vmem_limit_bytes=56 * 1024 * 1024),
        cost_estimate=pl.CostEstimate(flops=2 * 10**9, bytes_accessed=4 * 10**6, transcendentals=BLOCK * F),
    )(tile_rows, tile_cols, tile_counts, node_features, tile_values, cheb_weights, bias.reshape(1, F), out_cotangent)


def solution(mesh):
    return jax.shard_map(
        body,
        mesh=mesh,
        in_specs=(
            P(("section", "rep"), None),
            P(("section", "rep"), None, None),
            P(("section", "rep")),
            P(("section", "rep")),
            P(("section", "rep")),
            P(),
            P(),
            P(("section", "rep"), None),
        ),
        out_specs=(P(("section", "rep"), None), P()),
        check_vma=False,
    )
```

```python
import jax
import jax.numpy as jnp
from jax import lax
from jax.experimental import pallas as pl
from jax.experimental.pallas import tpu as pltpu
from jax.sharding import PartitionSpec as P

MESH = pl.DeviceIdType.MESH
N = 8
BLOCK = 128
F = 256
HALF = 128
TCAP = 16
BF16 = jnp.bfloat16
F32 = jnp.float32


RANK = (0, 1, 3, 5, 7, 6, 4, 2)
GROUPS = ((0, 1), (1, 3), (3, 5), (5, 7), (7, 8))
LINE = 0
ORDER = (
    (0, 1, LINE), (0, 0, 1), (0, 2, LINE), (1, 1, LINE), (1, 0, 1), (1, 2, LINE), (0, 0, 2), (0, 3, LINE), (0, 1, 1), (1, 0, 2),
    (0, 2, 1), (1, 3, LINE), (1, 1, 1), (1, 2, 1), (0, 0, 3), (0, 4, LINE), (0, 1, 2), (0, 3, 1), (1, 0, 3), (1, 4, LINE),
    (0, 2, 2), (0, 4, 1), (1, 3, 1), (1, 1, 2), (1, 2, 2), (1, 4, 1), (0, 3, 2), (0, 1, 3), (0, 4, 2), (0, 2, 3),
    (1, 3, 2), (1, 1, 3), (1, 4, 2), (1, 2, 3), (0, 3, 3), (0, 4, 3), (1, 3, 3), (1, 4, 3),
)
CHIPS = 4


def kernel(
    rows_ref, cols_ref, count_ref, x_hbm, tiles_hbm, w_hbm, bias_hbm, cot_hbm,
    out_ref, grad_ref,
    *scratch,
):
    gathers_a, gathers_b = scratch[0:4], scratch[4:8]
    partials, arrivals, own_sums = scratch[8:12], scratch[12:16], scratch[16:20]
    (x_ref, tiles_ref, w_ref, bias_ref, cot_ref, load_sem,
     adj, picked, hop1, hop2,
     grad_own, core_send, core_recv, x_send, x_recv, y_send, y_recv, z_all, y_all, rep_all,
     line_send, line_recv, ring_send, ring_recv, sum_send, sum_recv, red_send, red_recv) = scratch[20:]

    section = lax.axis_index("section")
    rep = lax.axis_index("rep")
    y = section // N
    z = section % N
    chip = rep // 2
    core = rep % 2
    other = 1 - core

    def ahead(pos, step):
        return lax.rem(pos + (step % N), N)

    def chip_ahead(step):
        return lax.rem(chip + step % CHIPS, CHIPS)

    def at_yz(yy, zz):
        return (yy * N + zz, rep)

    loads = [
        pltpu.make_async_copy(src, dst, load_sem.at[i])
        for i, (src, dst) in enumerate((
            (x_hbm, x_ref), (tiles_hbm, tiles_ref), (w_hbm, w_ref), (bias_hbm, bias_ref), (cot_hbm, cot_ref)))
    ]
    for load in loads:
        load.start()

    barrier = pltpu.get_barrier_semaphore()
    for d in range(1, N):
        for target in (at_yz(ahead(y, d), z), at_yz(y, ahead(z, d)), (section, ahead(rep, d))):
            pl.semaphore_signal(barrier, inc=1, device_id=target, device_id_type=MESH)

    loads[1].wait()

    def place(t, _):
        tile = tiles_ref[t]
        row = jnp.where(t < count_ref[0], rows_ref[t], N)
        for b in range(N):
            adj[b * BLOCK:(b + 1) * BLOCK, pl.ds(pl.multiple_of(t * BLOCK, BLOCK), BLOCK)] = jnp.where(
                row == b, tile, jnp.zeros_like(tile))
        return 0
    lax.fori_loop(0, TCAP, place, 0)
    for i in (0, 2, 3, 4):
        loads[i].wait()

    pl.semaphore_wait(barrier, 3 * (N - 1))

    def describe(src, dst, send_sem, recv_sem, target):
        return pltpu.make_async_remote_copy(
            src_ref=src, dst_ref=dst, send_sem=send_sem, recv_sem=recv_sem,
            device_id=target, device_id_type=MESH,
        )

    def remote(*args):
        describe(*args).start()

    sibling = (section, chip * 2 + other)

    def arrived(ref, sem):
        describe(ref, ref, sem, sem, sibling).wait_recv()

    def departed(ref, sem):
        describe(ref, ref, sem, sem, sibling).wait_send()

    orders = (
        (gathers_a, y, z, lambda u, v: at_yz(u, v)),
        (gathers_b, z, y, lambda u, v: at_yz(v, u)),
    )

    def line_put(stage, o, way, dist, hops):
        bufs, u, v, dev = orders[o]
        sign = 1 if way == 0 else -1
        remote(bufs[stage].at[u, RANK[-sign * (dist - hops) % N]], bufs[stage].at[u, RANK[-sign * dist % N]],
               line_send.at[stage, o], line_recv.at[stage, dist - 1], dev(u, ahead(v, sign * hops)))

    def ring_put(stage, g, k):
        for o, (bufs, u, v, dev) in enumerate(orders):
            for way, sign in ((0, 1), (1, -1)):
                first, last = GROUPS[g]
                if k == 4:
                    first, last = (first, min(last, 4)) if way == 0 else (max(first, 4), last)
                    if first >= last:
                        continue
                group = bufs[stage].at[ahead(u, -sign * (k - 1)), pl.ds(first, last - first)]
                remote(group, group, ring_send.at[stage, o], ring_recv.at[stage, g * 4 + k - 1], dev(ahead(u, sign), v))

    def ring_take(stage, g, k):
        first, last = GROUPS[g]
        arrived(gathers_a[stage].at[pl.ds(0, 2 if k == 4 else 4), pl.ds(first, last - first)],
                ring_recv.at[stage, g * 4 + k - 1])

    def gather_begin(stage, half):
        gathers_a[stage][y, 0] = half[:64]
        gathers_b[stage][z, 0] = half[64:]
        for dist in (1, 2):
            for o in (0, 1):
                for way in (0, 1):
                    line_put(stage, o, way, dist, dist)
        ring_put(stage, 0, 1)

    def gather_pair(base):
        for c, g, k in ORDER:
            stage = base + c
            if k == LINE:
                arrived(gathers_a[stage].at[pl.ds(0, 2 if g == 4 else 4), 0], line_recv.at[stage, g - 1])
                for o in (0, 1):
                    for way in (0, 1):
                        if g == 2 or (g == 3 and way == o):
                            line_put(stage, o, way, g + 1, 1)
                ring_put(stage, g, 1)
            else:
                ring_take(stage, g, k)
                ring_put(stage, g, k + 1)

    def gather_end(stage):
        for g in range(5):
            ring_take(stage, g, 4)

    def gather_departed(stage):
        for o, bufs in ((0, gathers_a), (1, gathers_b)):
            departed(bufs[stage].at[0, pl.ds(0, N - 1)], line_send.at[stage, o])
            departed(bufs[stage].at[pl.ds(0, N - 1)], ring_send.at[stage, o])
        departed(partials[stage].at[pl.ds(1, 3)], sum_send.at[stage, 1])
        departed(partials[stage].at[0, 0], sum_send.at[stage, 0])

    def multiply(stage):
        ga, gb = gathers_a[stage], gathers_b[stage]

        def rank(d):
            d = lax.rem(d + N, N)
            return jnp.where(d <= 4, jnp.maximum(2 * d - 1, 0), 2 * (N - d))

        def pick(t, _):
            col = cols_ref[t]
            cy, cz = lax.div(col, N), lax.rem(col, N)
            at = pl.multiple_of(t * BLOCK, BLOCK)
            picked[pl.ds(at, 64), :] = ga[cy, rank(cz - z)]
            picked[pl.ds(at + 64, 64), :] = gb[cz, rank(cy - y)]
            return 0
        lax.fori_loop(0, TCAP, pick, 0, unroll=4)

        for i in (2, 1, 3, 0):
            to = chip_ahead(i)
            product = jnp.dot(
                adj[pl.ds(pl.multiple_of(to * 256, 256), 256), :], picked[...], preferred_element_type=F32)
            partials[stage][i, 0] = product[:BLOCK].astype(BF16)
            partials[stage][i, 1] = product[BLOCK:].astype(BF16)
            if i:
                for c in (0, 1):
                    remote(partials[stage].at[i, c], arrivals[stage].at[i, core],
                           sum_send.at[stage, 1], sum_recv.at[stage, 1], (section, to * 2 + c))
            else:
                own_sums[stage][...] = jnp.where(core == 0, product[:BLOCK], product[BLOCK:])
                remote(partials[stage].at[0, other], arrivals[stage].at[0, 0],
                       sum_send.at[stage, 0], sum_recv.at[stage, 0], sibling)

    def total(stage):
        arrived(arrivals[stage].at[0, 0], sum_recv.at[stage, 0])
        acc = own_sums[stage][...] + arrivals[stage][0, 0].astype(F32)
        arrived(arrivals[stage].at[pl.ds(1, 3)], sum_recv.at[stage, 1])
        for i in (1, 2, 3):
            for c in (0, 1):
                acc += arrivals[stage][i, c].astype(F32)
        return acc

    def first_total(c):
        half = total(c).astype(BF16)
        hop1[:, c * HALF:(c + 1) * HALF] = half
        gather_begin(2 + c, half)

    def second_total(c):
        at = slice(c * HALF, (c + 1) * HALF)
        hop2[:, at] = (2.0 * total(2 + c) - x_ref[:, at].astype(F32)).astype(BF16)

    gather_begin(0, x_ref[:, :HALF])
    gather_begin(1, x_ref[:, HALF:])
    gather_pair(0)
    gather_end(0)
    multiply(0)
    gather_end(1)
    multiply(1)
    first_total(0)
    first_total(1)
    gather_pair(2)
    gather_end(2)
    multiply(2)
    gather_end(3)
    multiply(3)
    pre_act = jnp.dot(x_ref[...], w_ref[:F], preferred_element_type=F32)
    pre_act += jnp.dot(hop1[...], w_ref[F:2 * F], preferred_element_type=F32)
    pre_act += bias_ref[...]
    second_total(0)
    second_total(1)

    v = pre_act + jnp.dot(hop2[...], w_ref[2 * F:], preferred_element_type=F32)
    root = 0.7978845608028654
    th = jnp.tanh(root * (v + 0.044715 * (v * v * v)))
    cdf = 0.5 * (1.0 + th)
    slope = cdf + 0.5 * v * (1.0 - th * th) * (root * (1.0 + 3.0 * 0.044715 * (v * v)))
    pre_grad = (cot_ref[...].astype(F32) * slope).astype(BF16)

    def start(part, send, recv, src, dst, target):
        remote(src, dst, red_send.at[part, send], red_recv.at[part, recv], target)

    parts = range(3)
    others = (2, 1, 3)
    far = (4, 3, 5, 2, 6, 1, 7)
    for p, block in enumerate((x_ref, hop1, hop2)):
        local = lax.dot_general(block[...], pre_grad, (((0,), (0,)), ((), ())), preferred_element_type=F32)
        for i in range(8):
            value = local[i * 32:(i + 1) * 32]
            grad_own[p, i // CHIPS, i % CHIPS] = value
            core_send[p, i // CHIPS, i % CHIPS] = value.astype(BF16)
        start(p, 0, 0, core_send.at[p, other], core_recv.at[p], sibling)
    out_ref[...] = (v * cdf).astype(BF16)
    for p in parts:
        arrived(core_recv.at[p], red_recv.at[p, 0])
        for i in others:
            to = chip_ahead(i)
            x_send[p, i - 1] = (grad_own[p, core, to] + core_recv[p, to].astype(F32)).astype(BF16)
            start(p, 1, 1, x_send.at[p, i - 1], x_recv.at[p, i - 1], (section, to * 2 + core))
    gather_departed(0)
    gather_departed(1)
    for p in parts:
        acc = grad_own[p, core, chip] + core_recv[p, chip].astype(F32)
        arrived(x_recv.at[p], red_recv.at[p, 1])
        for i in range(CHIPS - 1):
            acc += x_recv[p, i].astype(F32)
        for i in range(N):
            y_send[p, i] = acc[(i // 2) * 8:(i // 2 + 1) * 8, (i % 2) * 128:(i % 2 + 1) * 128]
        for d in far:
            start(p, 2, 2, y_send.at[p, ahead(y, d)], y_recv.at[p, d - 1], at_yz(ahead(y, d), z))
    gather_departed(2)
    gather_departed(3)
    for p in parts:
        acc = y_send[p, y]
        arrived(y_recv.at[p], red_recv.at[p, 2])
        for d in range(1, N):
            acc += y_recv[p, d - 1]
        z_all[p, z] = acc
        for d in far:
            start(p, 3, 3, z_all.at[p, z], z_all.at[p, z], at_yz(y, ahead(z, d)))
    for p in parts:
        departed(core_send.at[p, 0], red_send.at[p, 0])
        departed(x_send.at[p], red_send.at[p, 1])
        departed(y_recv.at[p], red_send.at[p, 2])
    for p in parts:
        arrived(z_all.at[p, pl.ds(0, N - 1)], red_recv.at[p, 3])
        acc = z_all[p, 0]
        for i in range(1, N):
            acc += z_all[p, i]
        y_all[p, y] = acc
        for d in far:
            start(p, 4, 4, y_all.at[p, y], y_all.at[p, y], at_yz(ahead(y, d), z))
    for p in parts:
        departed(z_all.at[p, pl.ds(0, N - 1)], red_send.at[p, 3])
    for p in parts:
        arrived(y_all.at[p, pl.ds(0, N - 1)], red_recv.at[p, 4])
        rep_all[p, core, chip] = jnp.concatenate(
            [jnp.concatenate([y_all[p, 2 * i], y_all[p, 2 * i + 1]], axis=1) for i in range(4)], axis=0).astype(BF16)
        mine = rep_all.at[p, core, chip]
        for i in others:
            start(p, 5, 5 + i, mine, mine, (section, chip_ahead(i) * 2 + core))
        start(p, 6, 5, mine, mine, sibling)
    for p in parts:
        departed(y_all.at[p, pl.ds(0, N - 1)], red_send.at[p, 4])
    for p in parts:
        for i in (1, 3, 2):
            came = rep_all.at[p, core, chip_ahead(-i)]
            arrived(came, red_recv.at[p, 5 + i])
            start(p, 6, 5, came, came, sibling)
    for p in parts:
        arrived(rep_all.at[p, other], red_recv.at[p, 5])
        for i in range(N):
            at = p * F + i * 32
            grad_ref[at:at + 32, :] = rep_all[p, i // CHIPS, i % CHIPS].astype(F32)
    for p in parts:
        departed(rep_all.at[p, 0, pl.ds(0, CHIPS - 1)], red_send.at[p, 5])
        departed(rep_all.at[p, 0], red_send.at[p, 6])


def body(node_features, tile_values, tile_rows, tile_cols, tile_counts, cheb_weights, bias, out_cotangent):
    vmem = pl.BlockSpec(memory_space=pltpu.VMEM)
    smem = pl.BlockSpec(memory_space=pltpu.SMEM)
    anywhere = pl.BlockSpec(memory_space=pl.ANY)
    dma = pltpu.SemaphoreType.DMA
    scratch = (
        [pltpu.VMEM((N, N, 64, HALF), BF16)] * 8
        + [pltpu.VMEM((CHIPS, 2, BLOCK, HALF), BF16)] * 8
        + [pltpu.VMEM((BLOCK, HALF), F32)] * 4
        + [
            pltpu.VMEM((BLOCK, F), BF16),
            pltpu.VMEM((TCAP, BLOCK, BLOCK), BF16),
            pltpu.VMEM((3 * F, F), BF16),
            pltpu.VMEM((1, F), F32),
            pltpu.VMEM((BLOCK, F), BF16),
            dma((5,)),
            pltpu.VMEM((N * BLOCK, TCAP * BLOCK), BF16),
            pltpu.VMEM((TCAP * BLOCK, HALF), BF16),
            pltpu.VMEM((BLOCK, F), BF16),
            pltpu.VMEM((BLOCK, F), BF16),
            pltpu.VMEM((3, 2, CHIPS, 32, F), F32),
            pltpu.VMEM((3, 2, CHIPS, 32, F), BF16),
            pltpu.VMEM((3, CHIPS, 32, F), BF16),
            pltpu.VMEM((3, CHIPS - 1, 32, F), BF16),
            pltpu.VMEM((3, CHIPS - 1, 32, F), BF16),
            pltpu.VMEM((3, N, 8, 128), F32),
            pltpu.VMEM((3, N - 1, 8, 128), F32),
            pltpu.VMEM((3, N, 8, 128), F32),
            pltpu.VMEM((3, N, 8, 128), F32),
            pltpu.VMEM((3, 2, CHIPS, 32, F), BF16),
            dma((4, 2)), dma((4, 4)),
            dma((4, 2)), dma((4, 20)),
            dma((4, 2)), dma((4, 2)),
            dma((3, 7)), dma((3, 9)),
        ]
    )
    return pl.pallas_call(
        kernel,
        out_shape=(
            jax.ShapeDtypeStruct((BLOCK, F), BF16),
            jax.ShapeDtypeStruct((3 * F, F), F32),
        ),
        in_specs=[smem] * 3 + [anywhere] * 5,
        out_specs=(vmem, vmem),
        scratch_shapes=scratch,
        compiler_params=pltpu.CompilerParams(
            collective_id=0, has_side_effects=True, vmem_limit_bytes=56 * 1024 * 1024),
        cost_estimate=pl.CostEstimate(flops=2 * 10**9, bytes_accessed=4 * 10**6, transcendentals=BLOCK * F),
    )(tile_rows, tile_cols, tile_counts, node_features, tile_values, cheb_weights, bias.reshape(1, F), out_cotangent)


def solution(mesh):
    return jax.shard_map(
        body,
        mesh=mesh,
        in_specs=(
            P(("section", "rep"), None),
            P(("section", "rep"), None, None),
            P(("section", "rep")),
            P(("section", "rep")),
            P(("section", "rep")),
            P(),
            P(),
            P(("section", "rep"), None),
        ),
        out_specs=(P(("section", "rep"), None), P()),
        check_vma=False,
    )
```

```python
import jax
import jax.numpy as jnp
from jax import lax
from jax.experimental import pallas as pl
from jax.experimental.pallas import tpu as pltpu
from jax.sharding import PartitionSpec as P

MESH = pl.DeviceIdType.MESH
N = 8
BLOCK = 128
F = 256
HALF = 128
TCAP = 16
BF16 = jnp.bfloat16
F32 = jnp.float32


RANK = (0, 1, 3, 5, 7, 6, 4, 2)
GROUPS = ((0, 1), (1, 3), (3, 5), (5, 7), (7, 8))
LINE = 0
ORDER = (
    (0, 1, LINE), (0, 0, 1), (0, 2, LINE), (1, 1, LINE), (1, 0, 1), (1, 2, LINE), (0, 0, 2), (0, 3, LINE), (0, 1, 1), (1, 0, 2),
    (0, 2, 1), (1, 3, LINE), (1, 1, 1), (1, 2, 1), (0, 0, 3), (0, 4, LINE), (0, 1, 2), (0, 3, 1), (1, 0, 3), (1, 4, LINE),
    (0, 2, 2), (0, 4, 1), (1, 3, 1), (1, 1, 2), (1, 2, 2), (1, 4, 1), (0, 3, 2), (0, 1, 3), (0, 4, 2), (0, 2, 3),
    (1, 3, 2), (1, 1, 3), (1, 4, 2), (1, 2, 3), (0, 3, 3), (0, 4, 3), (1, 3, 3), (1, 4, 3),
)
CHIPS = 4


def kernel(
    rows_ref, cols_ref, count_ref, x_hbm, tiles_hbm, w_hbm, bias_hbm, cot_hbm,
    out_ref, grad_ref,
    *scratch,
):
    gathers_a, gathers_b = scratch[0:4], scratch[4:8]
    partials, arrivals, own_sums = scratch[8:12], scratch[12:16], scratch[16:20]
    (x_ref, tiles_ref, w_ref, bias_ref, cot_ref, load_sem,
     adj, picked, hop1, hop2,
     grad_own, core_send, core_recv, x_send, x_recv, y_send, y_recv, z_all, y_all, rep_all,
     line_send, line_recv, ring_send, ring_recv, sum_send, sum_recv, red_send, red_recv) = scratch[20:]

    section = lax.axis_index("section")
    rep = lax.axis_index("rep")
    y = section // N
    z = section % N
    chip = rep // 2
    core = rep % 2
    other = 1 - core

    def ahead(pos, step):
        return lax.rem(pos + (step % N), N)

    def chip_ahead(step):
        return lax.rem(chip + step % CHIPS, CHIPS)

    def at_yz(yy, zz):
        return (yy * N + zz, rep)

    loads = [
        pltpu.make_async_copy(src, dst, load_sem.at[i])
        for i, (src, dst) in enumerate((
            (x_hbm, x_ref), (tiles_hbm, tiles_ref), (w_hbm, w_ref), (bias_hbm, bias_ref), (cot_hbm, cot_ref)))
    ]
    for load in loads:
        load.start()

    barrier = pltpu.get_barrier_semaphore()
    near = [(section, ahead(rep, d)) for d in range(1, N)]
    for d in (1, 2, -1, -2):
        near += [at_yz(ahead(y, d), z), at_yz(y, ahead(z, d))]
    for target in near:
        pl.semaphore_signal(barrier, inc=1, device_id=target, device_id_type=MESH)

    loads[1].wait()

    def place(t, _):
        tile = tiles_ref[t]
        row = jnp.where(t < count_ref[0], rows_ref[t], N)
        for b in range(N):
            adj[b * BLOCK:(b + 1) * BLOCK, pl.ds(pl.multiple_of(t * BLOCK, BLOCK), BLOCK)] = jnp.where(
                row == b, tile, jnp.zeros_like(tile))
        return 0
    lax.fori_loop(0, TCAP, place, 0)
    for i in (0, 2, 3, 4):
        loads[i].wait()

    pl.semaphore_wait(barrier, len(near))

    def describe(src, dst, send_sem, recv_sem, target):
        return pltpu.make_async_remote_copy(
            src_ref=src, dst_ref=dst, send_sem=send_sem, recv_sem=recv_sem,
            device_id=target, device_id_type=MESH,
        )

    def remote(*args):
        describe(*args).start()

    sibling = (section, chip * 2 + other)

    def arrived(ref, sem):
        describe(ref, ref, sem, sem, sibling).wait_recv()

    def departed(ref, sem):
        describe(ref, ref, sem, sem, sibling).wait_send()

    orders = (
        (gathers_a, y, z, lambda u, v: at_yz(u, v)),
        (gathers_b, z, y, lambda u, v: at_yz(v, u)),
    )

    def line_put(stage, o, way, dist, hops):
        bufs, u, v, dev = orders[o]
        sign = 1 if way == 0 else -1
        remote(bufs[stage].at[u, RANK[-sign * (dist - hops) % N]], bufs[stage].at[u, RANK[-sign * dist % N]],
               line_send.at[stage, o], line_recv.at[stage, dist - 1], dev(u, ahead(v, sign * hops)))

    def ring_put(stage, g, k):
        for o, (bufs, u, v, dev) in enumerate(orders):
            for way, sign in ((0, 1), (1, -1)):
                first, last = GROUPS[g]
                if k == 4:
                    first, last = (first, min(last, 4)) if way == 0 else (max(first, 4), last)
                    if first >= last:
                        continue
                group = bufs[stage].at[ahead(u, -sign * (k - 1)), pl.ds(first, last - first)]
                remote(group, group, ring_send.at[stage, o], ring_recv.at[stage, g * 4 + k - 1], dev(ahead(u, sign), v))

    def ring_take(stage, g, k):
        first, last = GROUPS[g]
        arrived(gathers_a[stage].at[pl.ds(0, 2 if k == 4 else 4), pl.ds(first, last - first)],
                ring_recv.at[stage, g * 4 + k - 1])

    def gather_begin(stage, half):
        gathers_a[stage][y, 0] = half[:64]
        gathers_b[stage][z, 0] = half[64:]
        for dist in (1, 2):
            for o in (0, 1):
                for way in (0, 1):
                    line_put(stage, o, way, dist, dist)
        ring_put(stage, 0, 1)

    def gather_pair(base):
        for c, g, k in ORDER:
            stage = base + c
            if k == LINE:
                arrived(gathers_a[stage].at[pl.ds(0, 2 if g == 4 else 4), 0], line_recv.at[stage, g - 1])
                for o in (0, 1):
                    for way in (0, 1):
                        if g == 2 or (g == 3 and way == o):
                            line_put(stage, o, way, g + 1, 1)
                ring_put(stage, g, 1)
            else:
                ring_take(stage, g, k)
                ring_put(stage, g, k + 1)

    def gather_end(stage):
        for g in range(5):
            ring_take(stage, g, 4)

    def gather_departed(stage):
        for o, bufs in ((0, gathers_a), (1, gathers_b)):
            departed(bufs[stage].at[0, pl.ds(0, N - 1)], line_send.at[stage, o])
            departed(bufs[stage].at[pl.ds(0, N - 1)], ring_send.at[stage, o])
        departed(partials[stage].at[pl.ds(1, 3)], sum_send.at[stage, 1])
        departed(partials[stage].at[0, 0], sum_send.at[stage, 0])

    def multiply(stage):
        ga, gb = gathers_a[stage], gathers_b[stage]

        def rank(d):
            d = lax.rem(d + N, N)
            return jnp.where(d <= 4, jnp.maximum(2 * d - 1, 0), 2 * (N - d))

        def pick(t, _):
            col = cols_ref[t]
            cy, cz = lax.div(col, N), lax.rem(col, N)
            at = pl.multiple_of(t * BLOCK, BLOCK)
            picked[pl.ds(at, 64), :] = ga[cy, rank(cz - z)]
            picked[pl.ds(at + 64, 64), :] = gb[cz, rank(cy - y)]
            return 0
        lax.fori_loop(0, TCAP, pick, 0, unroll=4)

        for i in (2, 1, 3, 0):
            to = chip_ahead(i)
            product = jnp.dot(
                adj[pl.ds(pl.multiple_of(to * 256, 256), 256), :], picked[...], preferred_element_type=F32)
            partials[stage][i, 0] = product[:BLOCK].astype(BF16)
            partials[stage][i, 1] = product[BLOCK:].astype(BF16)
            if i:
                for c in (0, 1):
                    remote(partials[stage].at[i, c], arrivals[stage].at[i, core],
                           sum_send.at[stage, 1], sum_recv.at[stage, 1], (section, to * 2 + c))
            else:
                own_sums[stage][...] = jnp.where(core == 0, product[:BLOCK], product[BLOCK:])
                remote(partials[stage].at[0, other], arrivals[stage].at[0, 0],
                       sum_send.at[stage, 0], sum_recv.at[stage, 0], sibling)

    def total(stage):
        arrived(arrivals[stage].at[0, 0], sum_recv.at[stage, 0])
        acc = own_sums[stage][...] + arrivals[stage][0, 0].astype(F32)
        arrived(arrivals[stage].at[pl.ds(1, 3)], sum_recv.at[stage, 1])
        for i in (1, 2, 3):
            for c in (0, 1):
                acc += arrivals[stage][i, c].astype(F32)
        return acc

    def first_total(c):
        half = total(c).astype(BF16)
        hop1[:, c * HALF:(c + 1) * HALF] = half
        gather_begin(2 + c, half)

    def second_total(c):
        at = slice(c * HALF, (c + 1) * HALF)
        hop2[:, at] = (2.0 * total(2 + c) - x_ref[:, at].astype(F32)).astype(BF16)

    gather_begin(0, x_ref[:, :HALF])
    gather_begin(1, x_ref[:, HALF:])
    gather_pair(0)
    gather_end(0)
    multiply(0)
    gather_end(1)
    multiply(1)
    first_total(0)
    first_total(1)
    gather_pair(2)
    gather_end(2)
    multiply(2)
    gather_end(3)
    multiply(3)
    pre_act = jnp.dot(x_ref[...], w_ref[:F], preferred_element_type=F32)
    pre_act += jnp.dot(hop1[...], w_ref[F:2 * F], preferred_element_type=F32)
    pre_act += bias_ref[...]
    second_total(0)
    second_total(1)

    v = pre_act + jnp.dot(hop2[...], w_ref[2 * F:], preferred_element_type=F32)
    root = 0.7978845608028654
    th = jnp.tanh(root * (v + 0.044715 * (v * v * v)))
    cdf = 0.5 * (1.0 + th)
    slope = cdf + 0.5 * v * (1.0 - th * th) * (root * (1.0 + 3.0 * 0.044715 * (v * v)))
    pre_grad = (cot_ref[...].astype(F32) * slope).astype(BF16)

    def start(part, send, recv, src, dst, target):
        remote(src, dst, red_send.at[part, send], red_recv.at[part, recv], target)

    parts = range(3)
    others = (2, 1, 3)
    far = (4, 3, 5, 2, 6, 1, 7)
    for p, block in enumerate((x_ref, hop1, hop2)):
        local = lax.dot_general(block[...], pre_grad, (((0,), (0,)), ((), ())), preferred_element_type=F32)
        for i in range(8):
            value = local[i * 32:(i + 1) * 32]
            grad_own[p, i // CHIPS, i % CHIPS] = value
            core_send[p, i // CHIPS, i % CHIPS] = value.astype(BF16)
        start(p, 0, 0, core_send.at[p, other], core_recv.at[p], sibling)
    out_ref[...] = (v * cdf).astype(BF16)
    for p in parts:
        arrived(core_recv.at[p], red_recv.at[p, 0])
        for i in others:
            to = chip_ahead(i)
            x_send[p, i - 1] = (grad_own[p, core, to] + core_recv[p, to].astype(F32)).astype(BF16)
            start(p, 1, 1, x_send.at[p, i - 1], x_recv.at[p, i - 1], (section, to * 2 + core))
    gather_departed(0)
    gather_departed(1)
    for p in parts:
        acc = grad_own[p, core, chip] + core_recv[p, chip].astype(F32)
        arrived(x_recv.at[p], red_recv.at[p, 1])
        for i in range(CHIPS - 1):
            acc += x_recv[p, i].astype(F32)
        for i in range(N):
            y_send[p, i] = acc[(i // 2) * 8:(i // 2 + 1) * 8, (i % 2) * 128:(i % 2 + 1) * 128]
        for d in far:
            start(p, 2, 2, y_send.at[p, ahead(y, d)], y_recv.at[p, d - 1], at_yz(ahead(y, d), z))
    gather_departed(2)
    gather_departed(3)
    for p in parts:
        acc = y_send[p, y]
        arrived(y_recv.at[p], red_recv.at[p, 2])
        for d in range(1, N):
            acc += y_recv[p, d - 1]
        z_all[p, z] = acc
        for d in far:
            start(p, 3, 3, z_all.at[p, z], z_all.at[p, z], at_yz(y, ahead(z, d)))
    for p in parts:
        departed(core_send.at[p, 0], red_send.at[p, 0])
        departed(x_send.at[p], red_send.at[p, 1])
        departed(y_recv.at[p], red_send.at[p, 2])
    for p in parts:
        arrived(z_all.at[p, pl.ds(0, N - 1)], red_recv.at[p, 3])
        acc = z_all[p, 0]
        for i in range(1, N):
            acc += z_all[p, i]
        y_all[p, y] = acc
        for d in far:
            start(p, 4, 4, y_all.at[p, y], y_all.at[p, y], at_yz(ahead(y, d), z))
    for p in parts:
        departed(z_all.at[p, pl.ds(0, N - 1)], red_send.at[p, 3])
    for p in parts:
        arrived(y_all.at[p, pl.ds(0, N - 1)], red_recv.at[p, 4])
        rep_all[p, core, chip] = jnp.concatenate(
            [jnp.concatenate([y_all[p, 2 * i], y_all[p, 2 * i + 1]], axis=1) for i in range(4)], axis=0).astype(BF16)
        mine = rep_all.at[p, core, chip]
        for i in others:
            start(p, 5, 5 + i, mine, mine, (section, chip_ahead(i) * 2 + core))
        start(p, 6, 5, mine, mine, sibling)
    for p in parts:
        departed(y_all.at[p, pl.ds(0, N - 1)], red_send.at[p, 4])
    for p in parts:
        for i in (1, 3, 2):
            came = rep_all.at[p, core, chip_ahead(-i)]
            arrived(came, red_recv.at[p, 5 + i])
            start(p, 6, 5, came, came, sibling)
    for p in parts:
        arrived(rep_all.at[p, other], red_recv.at[p, 5])
        for i in range(N):
            at = p * F + i * 32
            grad_ref[at:at + 32, :] = rep_all[p, i // CHIPS, i % CHIPS].astype(F32)
    for p in parts:
        departed(rep_all.at[p, 0, pl.ds(0, CHIPS - 1)], red_send.at[p, 5])
        departed(rep_all.at[p, 0], red_send.at[p, 6])


def body(node_features, tile_values, tile_rows, tile_cols, tile_counts, cheb_weights, bias, out_cotangent):
    vmem = pl.BlockSpec(memory_space=pltpu.VMEM)
    smem = pl.BlockSpec(memory_space=pltpu.SMEM)
    anywhere = pl.BlockSpec(memory_space=pl.ANY)
    dma = pltpu.SemaphoreType.DMA
    scratch = (
        [pltpu.VMEM((N, N, 64, HALF), BF16)] * 8
        + [pltpu.VMEM((CHIPS, 2, BLOCK, HALF), BF16)] * 8
        + [pltpu.VMEM((BLOCK, HALF), F32)] * 4
        + [
            pltpu.VMEM((BLOCK, F), BF16),
            pltpu.VMEM((TCAP, BLOCK, BLOCK), BF16),
            pltpu.VMEM((3 * F, F), BF16),
            pltpu.VMEM((1, F), F32),
            pltpu.VMEM((BLOCK, F), BF16),
            dma((5,)),
            pltpu.VMEM((N * BLOCK, TCAP * BLOCK), BF16),
            pltpu.VMEM((TCAP * BLOCK, HALF), BF16),
            pltpu.VMEM((BLOCK, F), BF16),
            pltpu.VMEM((BLOCK, F), BF16),
            pltpu.VMEM((3, 2, CHIPS, 32, F), F32),
            pltpu.VMEM((3, 2, CHIPS, 32, F), BF16),
            pltpu.VMEM((3, CHIPS, 32, F), BF16),
            pltpu.VMEM((3, CHIPS - 1, 32, F), BF16),
            pltpu.VMEM((3, CHIPS - 1, 32, F), BF16),
            pltpu.VMEM((3, N, 8, 128), F32),
            pltpu.VMEM((3, N - 1, 8, 128), F32),
            pltpu.VMEM((3, N, 8, 128), F32),
            pltpu.VMEM((3, N, 8, 128), F32),
            pltpu.VMEM((3, 2, CHIPS, 32, F), BF16),
            dma((4, 2)), dma((4, 4)),
            dma((4, 2)), dma((4, 20)),
            dma((4, 2)), dma((4, 2)),
            dma((3, 7)), dma((3, 9)),
        ]
    )
    return pl.pallas_call(
        kernel,
        out_shape=(
            jax.ShapeDtypeStruct((BLOCK, F), BF16),
            jax.ShapeDtypeStruct((3 * F, F), F32),
        ),
        in_specs=[smem] * 3 + [anywhere] * 5,
        out_specs=(vmem, vmem),
        scratch_shapes=scratch,
        compiler_params=pltpu.CompilerParams(
            collective_id=0, has_side_effects=True, vmem_limit_bytes=56 * 1024 * 1024),
        cost_estimate=pl.CostEstimate(flops=2 * 10**9, bytes_accessed=4 * 10**6, transcendentals=BLOCK * F),
    )(tile_rows, tile_cols, tile_counts, node_features, tile_values, cheb_weights, bias.reshape(1, F), out_cotangent)


def solution(mesh):
    return jax.shard_map(
        body,
        mesh=mesh,
        in_specs=(
            P(("section", "rep"), None),
            P(("section", "rep"), None, None),
            P(("section", "rep")),
            P(("section", "rep")),
            P(("section", "rep")),
            P(),
            P(),
            P(("section", "rep"), None),
        ),
        out_specs=(P(("section", "rep"), None), P()),
        check_vma=False,
    )
```

```python
import jax
import jax.numpy as jnp
from jax import lax
from jax.experimental import pallas as pl
from jax.experimental.pallas import tpu as pltpu
from jax.sharding import PartitionSpec as P

MESH = pl.DeviceIdType.MESH
N = 8
BLOCK = 128
F = 256
HALF = 128
TCAP = 16
BF16 = jnp.bfloat16
F32 = jnp.float32


RANK = (0, 1, 3, 5, 7, 6, 4, 2)
GROUPS = ((0, 1), (1, 3), (3, 5), (5, 7), (7, 8))
LINE = 0
ORDER = (
    (0, 1, LINE), (0, 0, 1), (0, 2, LINE), (1, 1, LINE), (1, 0, 1), (1, 2, LINE), (0, 0, 2), (0, 3, LINE), (0, 1, 1), (1, 0, 2),
    (0, 2, 1), (1, 3, LINE), (1, 1, 1), (1, 2, 1), (0, 0, 3), (0, 4, LINE), (0, 1, 2), (0, 3, 1), (1, 0, 3), (1, 4, LINE),
    (0, 2, 2), (0, 4, 1), (1, 3, 1), (1, 1, 2), (1, 2, 2), (1, 4, 1), (0, 3, 2), (0, 1, 3), (0, 4, 2), (0, 2, 3),
    (1, 3, 2), (1, 1, 3), (1, 4, 2), (1, 2, 3), (0, 3, 3), (0, 4, 3), (1, 3, 3), (1, 4, 3),
)
CHIPS = 4


def kernel(
    rows_ref, cols_ref, count_ref, x_hbm, tiles_hbm, w_hbm, bias_hbm, cot_hbm,
    out_hbm, grad_hbm,
    *scratch,
):
    gathers_a, gathers_b = scratch[0:4], scratch[4:8]
    partials, arrivals, own_sums = scratch[8:12], scratch[12:16], scratch[16:20]
    (x_ref, tiles_ref, w_ref, bias_ref, cot_ref, load_sem,
     adj, picked, hop1, hop2, out_ref, grad_ref, store_sem,
     grad_own, core_send, core_recv, x_send, x_recv, y_send, y_recv, z_all, y_all, rep_all,
     line_send, line_recv, ring_send, ring_recv, sum_send, sum_recv, red_send, red_recv) = scratch[20:]

    section = lax.axis_index("section")
    rep = lax.axis_index("rep")
    y = section // N
    z = section % N
    chip = rep // 2
    core = rep % 2
    other = 1 - core

    def ahead(pos, step):
        return lax.rem(pos + (step % N), N)

    def chip_ahead(step):
        return lax.rem(chip + step % CHIPS, CHIPS)

    def at_yz(yy, zz):
        return (yy * N + zz, rep)

    loads = [
        pltpu.make_async_copy(src, dst, load_sem.at[i])
        for i, (src, dst) in enumerate((
            (x_hbm, x_ref), (tiles_hbm, tiles_ref), (w_hbm, w_ref), (bias_hbm, bias_ref), (cot_hbm, cot_ref)))
    ]
    for load in loads:
        load.start()

    barrier = pltpu.get_barrier_semaphore()
    near = [(section, ahead(rep, d)) for d in range(1, N)]
    for d in (1, 2, -1, -2):
        near += [at_yz(ahead(y, d), z), at_yz(y, ahead(z, d))]
    for target in near:
        pl.semaphore_signal(barrier, inc=1, device_id=target, device_id_type=MESH)

    loads[1].wait()

    def place(t, _):
        tile = tiles_ref[t]
        row = jnp.where(t < count_ref[0], rows_ref[t], N)
        for b in range(N):
            adj[b * BLOCK:(b + 1) * BLOCK, pl.ds(pl.multiple_of(t * BLOCK, BLOCK), BLOCK)] = jnp.where(
                row == b, tile, jnp.zeros_like(tile))
        return 0
    lax.fori_loop(0, TCAP, place, 0)
    for i in (0, 2, 3, 4):
        loads[i].wait()

    pl.semaphore_wait(barrier, len(near))

    def describe(src, dst, send_sem, recv_sem, target):
        return pltpu.make_async_remote_copy(
            src_ref=src, dst_ref=dst, send_sem=send_sem, recv_sem=recv_sem,
            device_id=target, device_id_type=MESH,
        )

    def remote(*args):
        describe(*args).start()

    sibling = (section, chip * 2 + other)

    def arrived(ref, sem):
        describe(ref, ref, sem, sem, sibling).wait_recv()

    def departed(ref, sem):
        describe(ref, ref, sem, sem, sibling).wait_send()

    orders = (
        (gathers_a, y, z, lambda u, v: at_yz(u, v)),
        (gathers_b, z, y, lambda u, v: at_yz(v, u)),
    )

    def line_put(stage, o, way, dist, hops):
        bufs, u, v, dev = orders[o]
        sign = 1 if way == 0 else -1
        remote(bufs[stage].at[u, RANK[-sign * (dist - hops) % N]], bufs[stage].at[u, RANK[-sign * dist % N]],
               line_send.at[stage, o], line_recv.at[stage, dist - 1], dev(u, ahead(v, sign * hops)))

    def ring_put(stage, g, k):
        for o, (bufs, u, v, dev) in enumerate(orders):
            for way, sign in ((0, 1), (1, -1)):
                first, last = GROUPS[g]
                if k == 4:
                    first, last = (first, min(last, 4)) if way == 0 else (max(first, 4), last)
                    if first >= last:
                        continue
                group = bufs[stage].at[ahead(u, -sign * (k - 1)), pl.ds(first, last - first)]
                remote(group, group, ring_send.at[stage, o], ring_recv.at[stage, g * 4 + k - 1], dev(ahead(u, sign), v))

    def ring_take(stage, g, k):
        first, last = GROUPS[g]
        arrived(gathers_a[stage].at[pl.ds(0, 2 if k == 4 else 4), pl.ds(first, last - first)],
                ring_recv.at[stage, g * 4 + k - 1])

    def gather_begin(stage, half):
        gathers_a[stage][y, 0] = half[:64]
        gathers_b[stage][z, 0] = half[64:]
        for dist in (1, 2):
            for o in (0, 1):
                for way in (0, 1):
                    line_put(stage, o, way, dist, dist)
        ring_put(stage, 0, 1)

    def gather_pair(base):
        for c, g, k in ORDER:
            stage = base + c
            if k == LINE:
                arrived(gathers_a[stage].at[pl.ds(0, 2 if g == 4 else 4), 0], line_recv.at[stage, g - 1])
                for o in (0, 1):
                    for way in (0, 1):
                        if g == 2 or (g == 3 and way == o):
                            line_put(stage, o, way, g + 1, 1)
                ring_put(stage, g, 1)
            else:
                ring_take(stage, g, k)
                ring_put(stage, g, k + 1)

    def gather_end(stage):
        for g in range(5):
            ring_take(stage, g, 4)

    def gather_departed(stage):
        for o, bufs in ((0, gathers_a), (1, gathers_b)):
            departed(bufs[stage].at[0, pl.ds(0, N - 1)], line_send.at[stage, o])
            departed(bufs[stage].at[pl.ds(0, N - 1)], ring_send.at[stage, o])
        departed(partials[stage].at[pl.ds(1, 3)], sum_send.at[stage, 1])
        departed(partials[stage].at[0, 0], sum_send.at[stage, 0])

    def multiply(stage):
        ga, gb = gathers_a[stage], gathers_b[stage]

        def rank(d):
            d = lax.rem(d + N, N)
            return jnp.where(d <= 4, jnp.maximum(2 * d - 1, 0), 2 * (N - d))

        def pick(t, _):
            col = cols_ref[t]
            cy, cz = lax.div(col, N), lax.rem(col, N)
            at = pl.multiple_of(t * BLOCK, BLOCK)
            picked[pl.ds(at, 64), :] = ga[cy, rank(cz - z)]
            picked[pl.ds(at + 64, 64), :] = gb[cz, rank(cy - y)]
            return 0
        lax.fori_loop(0, TCAP, pick, 0, unroll=4)

        for i in (2, 1, 3, 0):
            to = chip_ahead(i)
            product = jnp.dot(
                adj[pl.ds(pl.multiple_of(to * 256, 256), 256), :], picked[...], preferred_element_type=F32)
            partials[stage][i, 0] = product[:BLOCK].astype(BF16)
            partials[stage][i, 1] = product[BLOCK:].astype(BF16)
            if i:
                for c in (0, 1):
                    remote(partials[stage].at[i, c], arrivals[stage].at[i, core],
                           sum_send.at[stage, 1], sum_recv.at[stage, 1], (section, to * 2 + c))
            else:
                own_sums[stage][...] = jnp.where(core == 0, product[:BLOCK], product[BLOCK:])
                remote(partials[stage].at[0, other], arrivals[stage].at[0, 0],
                       sum_send.at[stage, 0], sum_recv.at[stage, 0], sibling)

    def total(stage):
        arrived(arrivals[stage].at[0, 0], sum_recv.at[stage, 0])
        acc = own_sums[stage][...] + arrivals[stage][0, 0].astype(F32)
        arrived(arrivals[stage].at[pl.ds(1, 3)], sum_recv.at[stage, 1])
        for i in (1, 2, 3):
            for c in (0, 1):
                acc += arrivals[stage][i, c].astype(F32)
        return acc

    def first_total(c):
        half = total(c).astype(BF16)
        hop1[:, c * HALF:(c + 1) * HALF] = half
        gather_begin(2 + c, half)

    def second_total(c):
        at = slice(c * HALF, (c + 1) * HALF)
        hop2[:, at] = (2.0 * total(2 + c) - x_ref[:, at].astype(F32)).astype(BF16)

    gather_begin(0, x_ref[:, :HALF])
    gather_begin(1, x_ref[:, HALF:])
    gather_pair(0)
    gather_end(0)
    multiply(0)
    gather_end(1)
    multiply(1)
    first_total(0)
    first_total(1)
    gather_pair(2)
    gather_end(2)
    multiply(2)
    gather_end(3)
    multiply(3)
    pre_act = jnp.dot(x_ref[...], w_ref[:F], preferred_element_type=F32)
    pre_act += jnp.dot(hop1[...], w_ref[F:2 * F], preferred_element_type=F32)
    pre_act += bias_ref[...]
    second_total(0)
    second_total(1)

    v = pre_act + jnp.dot(hop2[...], w_ref[2 * F:], preferred_element_type=F32)
    root = 0.7978845608028654
    th = jnp.tanh(root * (v + 0.044715 * (v * v * v)))
    cdf = 0.5 * (1.0 + th)
    slope = cdf + 0.5 * v * (1.0 - th * th) * (root * (1.0 + 3.0 * 0.044715 * (v * v)))
    pre_grad = (cot_ref[...].astype(F32) * slope).astype(BF16)

    def start(part, send, recv, src, dst, target):
        remote(src, dst, red_send.at[part, send], red_recv.at[part, recv], target)

    parts = range(3)
    others = (2, 1, 3)
    far = (4, 3, 5, 2, 6, 1, 7)
    for p, block in enumerate((x_ref, hop1, hop2)):
        local = lax.dot_general(block[...], pre_grad, (((0,), (0,)), ((), ())), preferred_element_type=F32)
        for i in range(8):
            value = local[i * 32:(i + 1) * 32]
            grad_own[p, i // CHIPS, i % CHIPS] = value
            core_send[p, i // CHIPS, i % CHIPS] = value.astype(BF16)
        start(p, 0, 0, core_send.at[p, other], core_recv.at[p], sibling)
    out_ref[...] = (v * cdf).astype(BF16)
    stores = [pltpu.make_async_copy(out_ref, out_hbm, store_sem.at[3])]
    stores[0].start()
    for p in parts:
        arrived(core_recv.at[p], red_recv.at[p, 0])
        for i in others:
            to = chip_ahead(i)
            x_send[p, i - 1] = (grad_own[p, core, to] + core_recv[p, to].astype(F32)).astype(BF16)
            start(p, 1, 1, x_send.at[p, i - 1], x_recv.at[p, i - 1], (section, to * 2 + core))
    gather_departed(0)
    gather_departed(1)
    for p in parts:
        acc = grad_own[p, core, chip] + core_recv[p, chip].astype(F32)
        arrived(x_recv.at[p], red_recv.at[p, 1])
        for i in range(CHIPS - 1):
            acc += x_recv[p, i].astype(F32)
        for i in range(N):
            y_send[p, i] = acc[(i // 2) * 8:(i // 2 + 1) * 8, (i % 2) * 128:(i % 2 + 1) * 128]
        for d in far:
            start(p, 2, 2, y_send.at[p, ahead(y, d)], y_recv.at[p, d - 1], at_yz(ahead(y, d), z))
    gather_departed(2)
    gather_departed(3)
    for p in parts:
        acc = y_send[p, y]
        arrived(y_recv.at[p], red_recv.at[p, 2])
        for d in range(1, N):
            acc += y_recv[p, d - 1]
        z_all[p, z] = acc
        for d in far:
            start(p, 3, 3, z_all.at[p, z], z_all.at[p, z], at_yz(y, ahead(z, d)))
    for p in parts:
        departed(core_send.at[p, 0], red_send.at[p, 0])
        departed(x_send.at[p], red_send.at[p, 1])
        departed(y_recv.at[p], red_send.at[p, 2])
    for p in parts:
        arrived(z_all.at[p, pl.ds(0, N - 1)], red_recv.at[p, 3])
        acc = z_all[p, 0]
        for i in range(1, N):
            acc += z_all[p, i]
        y_all[p, y] = acc
        for d in far:
            start(p, 4, 4, y_all.at[p, y], y_all.at[p, y], at_yz(ahead(y, d), z))
    for p in parts:
        departed(z_all.at[p, pl.ds(0, N - 1)], red_send.at[p, 3])
    for p in parts:
        arrived(y_all.at[p, pl.ds(0, N - 1)], red_recv.at[p, 4])
        rep_all[p, core, chip] = jnp.concatenate(
            [jnp.concatenate([y_all[p, 2 * i], y_all[p, 2 * i + 1]], axis=1) for i in range(4)], axis=0).astype(BF16)
        mine = rep_all.at[p, core, chip]
        for i in others:
            start(p, 5, 5 + i, mine, mine, (section, chip_ahead(i) * 2 + core))
        start(p, 6, 5, mine, mine, sibling)
    for p in parts:
        departed(y_all.at[p, pl.ds(0, N - 1)], red_send.at[p, 4])
    for p in parts:
        for i in (1, 3, 2):
            came = rep_all.at[p, core, chip_ahead(-i)]
            arrived(came, red_recv.at[p, 5 + i])
            start(p, 6, 5, came, came, sibling)
    for p in parts:
        arrived(rep_all.at[p, other], red_recv.at[p, 5])
        for i in range(N):
            at = p * F + i * 32
            grad_ref[at:at + 32, :] = rep_all[p, i // CHIPS, i % CHIPS].astype(F32)
        rows = pl.ds(p * F, F)
        stores.append(pltpu.make_async_copy(grad_ref.at[rows], grad_hbm.at[rows], store_sem.at[p]))
        stores[-1].start()
    for p in parts:
        departed(rep_all.at[p, 0, pl.ds(0, CHIPS - 1)], red_send.at[p, 5])
        departed(rep_all.at[p, 0], red_send.at[p, 6])
    for store in stores:
        store.wait()


def body(node_features, tile_values, tile_rows, tile_cols, tile_counts, cheb_weights, bias, out_cotangent):
    smem = pl.BlockSpec(memory_space=pltpu.SMEM)
    anywhere = pl.BlockSpec(memory_space=pl.ANY)
    dma = pltpu.SemaphoreType.DMA
    scratch = (
        [pltpu.VMEM((N, N, 64, HALF), BF16)] * 8
        + [pltpu.VMEM((CHIPS, 2, BLOCK, HALF), BF16)] * 8
        + [pltpu.VMEM((BLOCK, HALF), F32)] * 4
        + [
            pltpu.VMEM((BLOCK, F), BF16),
            pltpu.VMEM((TCAP, BLOCK, BLOCK), BF16),
            pltpu.VMEM((3 * F, F), BF16),
            pltpu.VMEM((1, F), F32),
            pltpu.VMEM((BLOCK, F), BF16),
            dma((5,)),
            pltpu.VMEM((N * BLOCK, TCAP * BLOCK), BF16),
            pltpu.VMEM((TCAP * BLOCK, HALF), BF16),
            pltpu.VMEM((BLOCK, F), BF16),
            pltpu.VMEM((BLOCK, F), BF16),
            pltpu.VMEM((BLOCK, F), BF16),
            pltpu.VMEM((3 * F, F), F32),
            dma((4,)),
            pltpu.VMEM((3, 2, CHIPS, 32, F), F32),
            pltpu.VMEM((3, 2, CHIPS, 32, F), BF16),
            pltpu.VMEM((3, CHIPS, 32, F), BF16),
            pltpu.VMEM((3, CHIPS - 1, 32, F), BF16),
            pltpu.VMEM((3, CHIPS - 1, 32, F), BF16),
            pltpu.VMEM((3, N, 8, 128), F32),
            pltpu.VMEM((3, N - 1, 8, 128), F32),
            pltpu.VMEM((3, N, 8, 128), F32),
            pltpu.VMEM((3, N, 8, 128), F32),
            pltpu.VMEM((3, 2, CHIPS, 32, F), BF16),
            dma((4, 2)), dma((4, 4)),
            dma((4, 2)), dma((4, 20)),
            dma((4, 2)), dma((4, 2)),
            dma((3, 7)), dma((3, 9)),
        ]
    )
    return pl.pallas_call(
        kernel,
        out_shape=(
            jax.ShapeDtypeStruct((BLOCK, F), BF16),
            jax.ShapeDtypeStruct((3 * F, F), F32),
        ),
        in_specs=[smem] * 3 + [anywhere] * 5,
        out_specs=(anywhere, anywhere),
        scratch_shapes=scratch,
        compiler_params=pltpu.CompilerParams(
            collective_id=0, has_side_effects=True, vmem_limit_bytes=56 * 1024 * 1024),
        cost_estimate=pl.CostEstimate(flops=2 * 10**9, bytes_accessed=4 * 10**6, transcendentals=BLOCK * F),
    )(tile_rows, tile_cols, tile_counts, node_features, tile_values, cheb_weights, bias.reshape(1, F), out_cotangent)


def solution(mesh):
    return jax.shard_map(
        body,
        mesh=mesh,
        in_specs=(
            P(("section", "rep"), None),
            P(("section", "rep"), None, None),
            P(("section", "rep")),
            P(("section", "rep")),
            P(("section", "rep")),
            P(),
            P(),
            P(("section", "rep"), None),
        ),
        out_specs=(P(("section", "rep"), None), P()),
        check_vma=False,
    )
```
